512 devices in a mesh: ctx: 64 (over z_hi, y, x), tp: 8 (over z_lo, core).
Axes of the slice: x: 4, y: 4, z: 16 (z_hi: 4, z_lo: 4; z = z_hi * 4 + z_lo), core: 2. Of those that a mesh axis runs over, the one named last changes fastest.
Arguments:
- query_gate: bfloat16 [4096, 8192], P('tp', 'ctx'), may hold values from -6 to 6
- key_gate: bfloat16 [4096, 8192], P('tp', 'ctx'), may hold values from -6 to 6
- value_input: bfloat16 [4096, 8192], P('tp', 'ctx'), may hold values from -6 to 6
- long_filter: float32 [4096, 8192], P('tp', 'ctx'), may hold values from -1.2 to 1.2
- skip_gain: float32 [4096], P('tp'), may hold values from -4 to 4
- out_weight: bfloat16 [4096, 4096], P('tp', 'ctx'), may hold values from -0.09375 to 0.09375
- out_bias: float32 [4096], P('tp'), may hold values from -3 to 3
Outputs:
- mixed_out: bfloat16 [4096, 8192], P('tp', 'ctx')
The draws below stay inside these ranges and needn't reach their ends.
All inputs are finite; a program needn't handle non-finite values.
Results may differ from the reference program's by a relative error of at most 0.0046.
Values may be sent and summed in bfloat16 or wider, within the bound.
A program may use at most 64 MiB of HBM per device.

```python
import math
import jax
import jax.numpy as jnp
from jax import lax

CH = 4096
SEQ = 8192


def draw_long_filter(key, part):
    key = jax.random.fold_in(key, 7)
    keys = jax.random.split(key, 9)
    lags = jnp.arange(SEQ, dtype=jnp.float32)[None, :]
    keep_share = 0.5
    slow_rows = jax.random.uniform(keys[0], (CH, 1)) < keep_share
    fast_length = jnp.exp(jax.random.uniform(keys[1], (CH, 1), minval=math.log(30.0), maxval=math.log(50.0)))
    slow_length = SEQ * jnp.exp(jax.random.uniform(keys[2], (CH, 1), minval=math.log(2.0), maxval=math.log(8.0)))
    decay_length = jnp.where(slow_rows, slow_length, fast_length)
    envelope = jnp.exp(-lags / decay_length)
    spots = jax.random.uniform(keys[3], (CH, 2)) * SEQ
    drops = jax.random.uniform(keys[4], (CH, 2), minval=0.5, maxval=0.8)
    envelope = envelope * jnp.where(lags >= spots[:, 0:1], drops[:, 0:1], 1.0)
    envelope = envelope * jnp.where(lags >= spots[:, 1:2], drops[:, 1:2], 1.0)
    scaling = 1.0 / jnp.sqrt(jnp.minimum(decay_length / 2.0, float(SEQ)))
    tail_share = jnp.exp(jax.random.uniform(keys[7], (CH, 1), minval=math.log(0.015), maxval=math.log(0.06)))
    tail_envelope = jnp.exp(-lags / slow_length) * jnp.sqrt(tail_share / float(SEQ))
    rough = jax.random.truncated_normal(keys[5], -4.0, 4.0, (CH, SEQ))
    tail_noise = jax.random.truncated_normal(keys[8], -4.0, 4.0, (CH, SEQ))
    head = rough * envelope * scaling
    tail = jnp.where(slow_rows, 0.0, tail_noise * tail_envelope)
    return (head + tail).astype(jnp.float32)


def level_of(stream_key, extent, cuts, least, high):
    level = 1.0
    for axis_at, blocks in cuts:
        heights = jax.random.uniform(jax.random.fold_in(jax.random.fold_in(stream_key, 6), axis_at), (blocks,), jnp.float32, least / len(cuts), high / len(cuts))
        level = level * jnp.repeat(jnp.exp(heights), extent[axis_at] // blocks).reshape((-1,) + (1,) * (len(extent) - 1 - axis_at))
    return level


def scatter_about(own_key, extent, deviation, most, cuts=(), kind=jnp.bfloat16):
    result = deviation * jax.random.normal(own_key, extent, jnp.float32)
    if cuts:
        result = result * level_of(own_key, extent, cuts, -0.22, 0.18)
    return jnp.clip(result, -most, most).astype(kind)


def setup_inputs(seed: int = 0) -> dict:
    key_list = jax.random.split(jax.random.key(seed), 8)
    query_gate = scatter_about(key_list[0], (CH, SEQ), 1.0, 6.0, ((0, 8), (1, 64)))
    key_gate = scatter_about(key_list[1], (CH, SEQ), 1.0, 6.0, ((0, 8), (1, 64)))
    value_input = scatter_about(key_list[2], (CH, SEQ), 1.0, 6.0, ((0, 8), (1, 64)))
    long_filter = draw_long_filter(jax.random.fold_in(key_list[7], 71), 0)
    skip_gain = scatter_about(key_list[4], (CH,), 1.0, 4.0, ((0, 8),), jnp.float32)
    out_weight = scatter_about(key_list[5], (CH, CH), CH ** -0.5, 0.09375, ((0, 8), (1, 64)))
    out_bias = scatter_about(key_list[6], (CH,), 0.5, 3.0, ((0, 8),), jnp.float32)
    return dict(query_gate=query_gate, key_gate=key_gate, value_input=value_input, long_filter=long_filter, skip_gain=skip_gain, out_weight=out_weight, out_bias=out_bias)


def convolve_group(operands):
    filter_rows, product_rows = operands
    spectrum = jnp.fft.rfft(filter_rows, n=2 * SEQ, axis=1) * jnp.fft.rfft(product_rows, n=2 * SEQ, axis=1)
    return jnp.fft.irfft(spectrum, n=2 * SEQ, axis=1)[:, :SEQ]


def reference(query_gate, key_gate, value_input, long_filter, skip_gain, out_weight, out_bias):
    products = key_gate.astype(jnp.float32) * value_input.astype(jnp.float32)
    groups = CH // 16
    filter_groups = long_filter.reshape(groups, 16, SEQ)
    product_groups = products.reshape(groups, 16, SEQ)
    long_conv = lax.map(convolve_group, (filter_groups, product_groups)).reshape(CH, SEQ)
    long_conv = long_conv + skip_gain[:, None] * products
    gated_values = (query_gate.astype(jnp.float32) * long_conv).astype(jnp.bfloat16)
    mixed_out = lax.dot_general(out_weight, gated_values, (((0,), (0,)), ((), ())), preferred_element_type=jnp.float32)
    return (mixed_out + out_bias[:, None]).astype(jnp.bfloat16)
```

```python
import functools

import jax
import jax.numpy as jnp
import numpy as np
from jax import lax
from jax.experimental import pallas as pl
from jax.experimental.pallas import tpu as pltpu
from jax.sharding import PartitionSpec as P

F32 = jnp.float32
BF16 = jnp.bfloat16
MESH = pl.DeviceIdType.MESH
LANES = 128
GROUP = 8


def split_bf16(array):
    high = array.astype(BF16)
    low = (array - np.asarray(high, np.float64)).astype(BF16)
    return np.asarray(high), np.asarray(low)


def transform_tables(blocks):
    n1 = np.arange(blocks)[:, None]
    k1 = np.arange(blocks)[None, :] + 0.5
    outer = 2.0 * np.pi * n1 * k1 / (2 * blocks)
    first = np.concatenate([np.cos(outer).T, -np.sin(outer).T], 0)
    first_hi, first_lo = split_bf16(first)
    scale = 2.0 / (2 * blocks * LANES)
    last = np.concatenate([np.cos(outer), -np.sin(outer)], 1) * scale
    last_hi, last_lo = split_bf16(last)
    lane = np.arange(LANES)
    inner = 2.0 * np.pi * (lane[:, None] * lane[None, :] % LANES) / LANES
    cos_part, sin_part = np.cos(inner), -np.sin(inner)
    forward = np.block([[cos_part, sin_part], [-sin_part, cos_part]])
    backward = np.block([[cos_part, -sin_part], [sin_part, cos_part]])
    turn = 2.0 * np.pi * k1.T * lane[None, :] / (2 * blocks * LANES)
    return (
        np.concatenate([first_hi, first_lo], 1),
        np.stack(split_bf16(forward)),
        np.stack(split_bf16(backward)),
        np.concatenate([last_hi, last_lo, last_hi], 1),
        np.stack([np.cos(turn), -np.sin(turn)]).astype(np.float32),
    )


def dot(left, right):
    return jnp.dot(left, right, preferred_element_type=F32)


def halves(value):
    high = value.astype(BF16)
    return high, (value - high.astype(F32)).astype(BF16)


def dot_split(value, table_ref):
    high, low = halves(value)
    return dot(high, table_ref[0]) + dot(low, table_ref[0]) + dot(high, table_ref[1])


def column(row, targets):
    lanes = lax.broadcasted_iota(jnp.int32, (targets.shape[0], row.shape[1]), 1)
    return jnp.sum(jnp.where(lanes == targets, row, 0.0), axis=1, keepdims=True)


def kernel(
    dims,
    q_ref,
    k_ref,
    v_ref,
    h_ref,
    skip_ref,
    w_ref,
    bias_ref,
    first_ref,
    fwd_ref,
    bwd_ref,
    last_ref,
    turn_ref,
    out_ref,
    cut,
    rows_in,
    query_in,
    seq_in,
    wide,
    conv_out,
    conv_wide,
    conv_in,
    gated,
    weights,
    pair_out,
    pair_in,
    own_sum,
    line_out,
    line_in,
    final,
    x_send,
    x_recv,
    q_send,
    q_recv,
    m_send,
    m_recv,
    wz_send,
    wz_recv,
    wy_send,
    wy_recv,
    r_send,
    r_recv,
    g_send,
    g_recv,
    c_send,
    c_recv,
    l_send,
    l_recv,
    e_send,
    e_recv,
):
    zh_n, y_n, x_n, zl_n = dims
    m_n = zh_n * y_n
    blocks = m_n * x_n
    me = lax.axis_index("ctx")
    tp = lax.axis_index("tp")
    x = me % x_n
    m = me // x_n
    y = m % y_n
    zh = m // y_n
    core = tp % 2
    zl = tp // 2
    channels = k_ref.shape[0]
    share = channels // x_n
    per_tp = m_n // (2 * zl_n)
    width = w_ref.shape[1]

    def at_x(step):
        return {"ctx": m * x_n + (x + step) % x_n, "tp": tp}

    def at_m(step):
        return {"ctx": (m + step) % m_n * x_n + x, "tp": tp}

    def at_zh(step):
        return {"ctx": ((zh + step) % zh_n * y_n + y) * x_n + x, "tp": tp}

    def at_y(step):
        return {"ctx": (zh * y_n + (y + step) % y_n) * x_n + x, "tp": tp}

    def at_zl(step):
        return {"ctx": me, "tp": (zl + step) % zl_n * 2 + core}

    other_core = {"ctx": me, "tp": zl * 2 + 1 - core}

    def remote(src, dst, send, recv, device):
        return pltpu.make_async_remote_copy(
            src_ref=src, dst_ref=dst, send_sem=send, recv_sem=recv, device_id=device, device_id_type=MESH
        )

    barrier = pltpu.get_barrier_semaphore()

    def greet(device):
        pl.semaphore_signal(barrier, inc=1, device_id=device, device_id_type=MESH)

    for step in range(1, x_n):
        greet(at_x(step))
    for step in range(1, m_n):
        greet(at_m(step))
    for step in range(1, zl_n):
        greet(at_zl(step))
    greet(other_core)

    products = k_ref[...].astype(F32) * v_ref[...].astype(F32)
    pieces = jnp.concatenate(
        [products.reshape(blocks, GROUP, LANES), h_ref[...].reshape(blocks, GROUP, LANES)], 1
    ).astype(BF16)
    cut[...] = pieces.reshape(x_n, m_n, 2 * GROUP, LANES)
    weights[m] = jnp.transpose(w_ref[...].astype(F32)).astype(BF16)
    own_rows = pl.ds(pl.multiple_of(x * share, share), share)
    index = lax.broadcasted_iota(jnp.int32, (share, 1), 0)
    skip = column(skip_ref[...], x * share + index)
    index = lax.broadcasted_iota(jnp.int32, (per_tp * width, 1), 0)
    bias = column(bias_ref[...], (index // width * x_n + x) * width + index % width)

    pl.semaphore_wait(barrier, (x_n - 1) + (m_n - 1) + (zl_n - 1) + 1)

    x_copies = []
    for step in range(1, x_n):
        copy = remote(
            cut.at[(x + step) % x_n], rows_in.at[:, x], x_send.at[step], x_recv.at[step], at_x(step)
        )
        copy.start()
        x_copies.append(copy)
    rows_in[:, pl.ds(x, 1)] = cut[pl.ds(x, 1)].reshape(m_n, 1, 2 * GROUP, LANES)
    query_in[pl.ds(x, 1)] = q_ref[own_rows, :][None]
    for copy in x_copies:
        copy.wait_recv()

    m_copies = []
    for step in range(1, m_n):
        copy = remote(
            rows_in.at[(m + step) % m_n], seq_in.at[m], m_send.at[step], m_recv.at[step], at_m(step)
        )
        copy.start()
        m_copies.append(copy)
    seq_in[m] = rows_in[m]
    q_copies = []
    for step in range(1, x_n):
        rows = pl.ds(pl.multiple_of((x + step) % x_n * share, share), share)
        copy = remote(q_ref.at[rows], query_in.at[x], q_send.at[step], q_recv.at[step], at_x(step))
        copy.start()
        q_copies.append(copy)
    wz_copies = []
    for step in range(1, zh_n):
        copy = remote(weights.at[m], weights.at[m], wz_send.at[step], wz_recv.at[step], at_zh(step))
        copy.start()
        wz_copies.append(copy)
    for copy in m_copies:
        copy.wait_recv()

    wide[...] = seq_in[...].reshape(blocks * 2 * GROUP, LANES).astype(F32)
    turn_re = turn_ref[0]
    turn_im = turn_ref[1]
    turn_re2 = jnp.concatenate([turn_re, turn_re], 1)
    turn_im2 = jnp.concatenate([turn_im, turn_im], 1)
    for channel in range(GROUP):
        signal = wide[pl.ds(channel, blocks, stride=2 * GROUP), :].astype(BF16)
        taps = wide[pl.ds(GROUP + channel, blocks, stride=2 * GROUP), :].astype(BF16)
        both = jnp.concatenate([signal, taps], 1)
        spread = dot(first_ref[...], jnp.concatenate([both, both], 0))
        re, im = spread[:blocks], spread[blocks:]
        turned_re = re * turn_re2 - im * turn_im2
        turned_im = re * turn_im2 + im * turn_re2
        stacked = jnp.concatenate(
            [
                jnp.concatenate([turned_re[:, :LANES], turned_im[:, :LANES]], 1),
                jnp.concatenate([turned_re[:, LANES:], turned_im[:, LANES:]], 1),
            ],
            0,
        )
        spectra = dot_split(stacked, fwd_ref)
        s_re, s_im = spectra[:blocks, :LANES], spectra[:blocks, LANES:]
        t_re, t_im = spectra[blocks:, :LANES], spectra[blocks:, LANES:]
        mixed = jnp.concatenate([s_re * t_re - s_im * t_im, s_re * t_im + s_im * t_re], 1)
        back = dot_split(mixed, bwd_ref)
        b_re, b_im = back[:, :LANES], back[:, LANES:]
        unturned = jnp.concatenate([b_re * turn_re + b_im * turn_im, b_im * turn_re - b_re * turn_im], 0)
        high, low = halves(unturned)
        conv_wide[pl.ds(channel, blocks, stride=GROUP), :] = dot(
            last_ref[...], jnp.concatenate([high, high, low], 0)
        )
    conv_out[...] = conv_wide[...].astype(BF16).reshape(m_n, x_n * GROUP, LANES)

    r_copies = []
    for step in range(1, m_n):
        copy = remote(
            conv_out.at[(m + step) % m_n], conv_in.at[m], r_send.at[step], r_recv.at[step], at_m(step)
        )
        copy.start()
        r_copies.append(copy)
    conv_in[m] = conv_out[m]
    for copy in wz_copies:
        copy.wait_recv()
    wy_copies = []
    for step in range(1, y_n):
        for part in range(zh_n):
            block = part * y_n + y
            copy = remote(
                weights.at[block],
                weights.at[block],
                wy_send.at[step, part],
                wy_recv.at[step, part],
                at_y(step),
            )
            copy.start()
            wy_copies.append(copy)
    for copy in q_copies:
        copy.wait_recv()
    for copy in r_copies:
        copy.wait_recv()

    conv = conv_in[...].astype(F32).reshape(m_n, x_n, GROUP, LANES)
    rows = rows_in[...].astype(F32)[:, :, :GROUP]
    for part in range(x_n):
        long_conv = conv[:, part].reshape(share, LANES) + skip * rows[:, part].reshape(share, LANES)
        gated[own_rows, part * LANES : (part + 1) * LANES] = (
            query_in[part].astype(F32) * long_conv
        ).astype(BF16)

    g_copies = []
    for step in range(1, x_n):
        copy = remote(gated.at[own_rows], gated.at[own_rows], g_send.at[step], g_recv.at[step], at_x(step))
        copy.start()
        g_copies.append(copy)
    for copy in wy_copies:
        copy.wait_recv()
    for copy in g_copies:
        copy.wait_recv()

    def project(target):
        block = weights[pl.ds(target * per_tp, per_tp)].reshape(per_tp * width, channels)
        return dot(block, gated[...])

    c_copies = []
    for step in range(zl_n):
        line = (zl + step + 1) % zl_n
        pair_out[step] = project(line * 2 + 1 - core)
        copy = remote(pair_out.at[step], pair_in.at[step], c_send.at[step], c_recv.at[step], other_core)
        copy.start()
        c_copies.append(copy)
    for step in range(zl_n):
        own_sum[step] = project((zl + step + 1) % zl_n * 2 + core)
    l_copies = []
    for step in range(1, zl_n):
        c_copies[step - 1].wait_recv()
        line_out[step] = (own_sum[step - 1] + pair_in[step - 1]).astype(BF16)
        copy = remote(line_out.at[step], line_in.at[step], l_send.at[step], l_recv.at[step], at_zl(step))
        copy.start()
        l_copies.append(copy)
    c_copies[zl_n - 1].wait_recv()
    total = own_sum[zl_n - 1] + pair_in[zl_n - 1] + bias
    for step in range(1, zl_n):
        l_copies[step - 1].wait_recv()
        total = total + line_in[step].astype(F32)
    total = total.astype(BF16)
    for part in range(x_n):
        final[part] = total[:, part * LANES : (part + 1) * LANES].reshape(per_tp, width, LANES)
    e_copies = []
    for step in range(1, x_n):
        copy = remote(
            final.at[(x + step) % x_n], out_ref.at[:, x], e_send.at[step], e_recv.at[step], at_x(step)
        )
        copy.start()
        e_copies.append(copy)
    out_ref[:, pl.ds(x, 1)] = final[pl.ds(x, 1)].reshape(per_tp, 1, width, LANES)
    for copy in e_copies:
        copy.wait_recv()
    for copies in (x_copies, m_copies, q_copies, wz_copies, r_copies, wy_copies, g_copies, c_copies, l_copies):
        for copy in copies:
            copy.wait_send()
    for copy in e_copies:
        copy.wait_send()


def on_device(dims, query_gate, key_gate, value_input, long_filter, skip_gain, out_weight, out_bias):
    zh_n, y_n, x_n, zl_n = dims
    m_n = zh_n * y_n
    blocks = m_n * x_n
    channels, length = key_gate.shape
    width = out_weight.shape[1]
    share = channels // x_n
    per_tp = m_n // (2 * zl_n)
    tables = [jnp.asarray(table) for table in transform_tables(blocks)]
    block_rows = per_tp * width
    span = x_n * LANES
    dma = pltpu.SemaphoreType.DMA
    out = pl.pallas_call(
        functools.partial(kernel, dims),
        out_shape=jax.ShapeDtypeStruct((per_tp, x_n, width, LANES), BF16),
        in_specs=[pl.BlockSpec(memory_space=pltpu.VMEM)] * 12,
        out_specs=pl.BlockSpec(memory_space=pltpu.VMEM),
        scratch_shapes=[
            pltpu.VMEM((x_n, m_n, 2 * GROUP, LANES), BF16),
            pltpu.VMEM((m_n, x_n, 2 * GROUP, LANES), BF16),
            pltpu.VMEM((x_n, share, LANES), BF16),
            pltpu.VMEM((m_n, x_n, 2 * GROUP, LANES), BF16),
            pltpu.VMEM((blocks * 2 * GROUP, LANES), F32),
            pltpu.VMEM((m_n, x_n * GROUP, LANES), BF16),
            pltpu.VMEM((blocks * GROUP, LANES), F32),
            pltpu.VMEM((m_n, x_n * GROUP, LANES), BF16),
            pltpu.VMEM((channels, span), BF16),
            pltpu.VMEM((m_n, width, channels), BF16),
            pltpu.VMEM((zl_n, block_rows, span), F32),
            pltpu.VMEM((zl_n, block_rows, span), F32),
            pltpu.VMEM((zl_n, block_rows, span), F32),
            pltpu.VMEM((zl_n, block_rows, span), BF16),
            pltpu.VMEM((zl_n, block_rows, span), BF16),
            pltpu.VMEM((x_n, per_tp, width, LANES), BF16),
            dma((x_n,)),
            dma((x_n,)),
            dma((x_n,)),
            dma((x_n,)),
            dma((m_n,)),
            dma((m_n,)),
            dma((zh_n,)),
            dma((zh_n,)),
            dma((y_n, zh_n)),
            dma((y_n, zh_n)),
            dma((m_n,)),
            dma((m_n,)),
            dma((x_n,)),
            dma((x_n,)),
            dma((zl_n,)),
            dma((zl_n,)),
            dma((zl_n,)),
            dma((zl_n,)),
            dma((x_n,)),
            dma((x_n,)),
        ],
        compiler_params=pltpu.CompilerParams(
            collective_id=0, has_side_effects=True, vmem_limit_bytes=48 * 1024 * 1024
        ),
        name="hyena_mixer",
    )(
        query_gate,
        key_gate,
        value_input,
        long_filter,
        skip_gain.reshape(1, channels),
        out_weight,
        out_bias.reshape(1, -1),
        *tables,
    )
    return out.reshape(per_tp * x_n * width, LANES)


def solution(mesh, dims=(4, 4, 4, 4)):
    placed = (
        P("tp", "ctx"),
        P("tp", "ctx"),
        P("tp", "ctx"),
        P("tp", "ctx"),
        P("tp"),
        P("tp", "ctx"),
        P("tp"),
    )
    return jax.shard_map(
        functools.partial(on_device, dims),
        mesh=mesh,
        in_specs=placed,
        out_specs=P("tp", "ctx"),
        check_vma=False,
    )
```

```python
import functools

import jax
import jax.numpy as jnp
import numpy as np
from jax import lax
from jax.experimental import pallas as pl
from jax.experimental.pallas import tpu as pltpu
from jax.sharding import PartitionSpec as P

F32 = jnp.float32
BF16 = jnp.bfloat16
MESH = pl.DeviceIdType.MESH
LANES = 128
GROUP = 8


def split_bf16(array):
    high = array.astype(BF16)
    low = (array - np.asarray(high, np.float64)).astype(BF16)
    return np.asarray(high), np.asarray(low)


def transform_tables(blocks):
    n1 = np.arange(blocks)[:, None]
    k1 = np.arange(blocks)[None, :] + 0.5
    outer = 2.0 * np.pi * n1 * k1 / (2 * blocks)
    first = np.concatenate([np.cos(outer).T, -np.sin(outer).T], 0)
    first_hi, first_lo = split_bf16(first)
    scale = 2.0 / (2 * blocks * LANES)
    last = np.concatenate([np.cos(outer), -np.sin(outer)], 1) * scale
    last_hi, last_lo = split_bf16(last)
    lane = np.arange(LANES)
    inner = 2.0 * np.pi * (lane[:, None] * lane[None, :] % LANES) / LANES
    cos_part, sin_part = np.cos(inner), -np.sin(inner)
    forward = np.block([[cos_part, sin_part], [-sin_part, cos_part]])
    backward = np.block([[cos_part, -sin_part], [sin_part, cos_part]])
    turn = 2.0 * np.pi * k1.T * lane[None, :] / (2 * blocks * LANES)
    return (
        np.concatenate([first_hi, first_lo], 1),
        np.stack(split_bf16(forward)),
        np.stack(split_bf16(backward)),
        np.concatenate([last_hi, last_lo, last_hi], 1),
        np.stack([np.cos(turn), -np.sin(turn)]).astype(np.float32),
    )


def dot(left, right):
    return jnp.dot(left, right, preferred_element_type=F32)


def halves(value):
    high = value.astype(BF16)
    return high, (value - high.astype(F32)).astype(BF16)


def dot_split(value, table_ref):
    high, low = halves(value)
    return dot(high, table_ref[0]) + dot(low, table_ref[0]) + dot(high, table_ref[1])


def column(row, targets):
    lanes = lax.broadcasted_iota(jnp.int32, (targets.shape[0], row.shape[1]), 1)
    return jnp.sum(jnp.where(lanes == targets, row, 0.0), axis=1, keepdims=True)


def kernel(
    dims,
    q_hbm,
    k_hbm,
    v_hbm,
    h_hbm,
    skip_hbm,
    w_hbm,
    bias_hbm,
    first_hbm,
    fwd_hbm,
    bwd_hbm,
    last_hbm,
    turn_hbm,
    out_ref,
    k_ref,
    v_ref,
    h_ref,
    skip_ref,
    bias_ref,
    first_ref,
    fwd_ref,
    bwd_ref,
    last_ref,
    turn_ref,
    cut,
    rows_in,
    query_in,
    seq_in,
    wide,
    conv_wide,
    conv_out,
    conv_in,
    gated_out,
    gated,
    w_line,
    weights,
    pair_out,
    pair_in,
    own_sum,
    sum_out,
    sum_in,
    load_sem,
    s_send,
    s_recv,
    q_send,
    q_recv,
    z_send,
    z_recv,
    wz_send,
    wz_recv,
    wp_send,
    wp_recv,
    r_send,
    r_recv,
    g_send,
    g_recv,
    c_send,
    c_recv,
    e_send,
    e_recv,
):
    zh_n, y_n, x_n, zl_n = dims
    plane = y_n * x_n
    blocks = zh_n * plane
    me = lax.axis_index("ctx")
    tp = lax.axis_index("tp")
    place = me % plane
    x = me % x_n
    y = place // x_n
    zh = me // plane
    core = tp % 2
    zl = tp // 2
    channels = k_hbm.shape[0]
    x_share = channels // x_n
    share = channels // plane
    width = w_hbm.shape[0]

    def device(zh_at, y_at, x_at, zl_at):
        return {"ctx": (zh_at * y_n + y_at) * x_n + x_at, "tp": zl_at * 2 + core}

    def in_plane(step):
        return {"ctx": zh * plane + (place + step) % plane, "tp": tp}

    def at_zh(step):
        return device((zh + step) % zh_n, y, x, zl)

    def at_x(step):
        return device(zh, y, (x + step) % x_n, zl)

    def at_y(step):
        return device(zh, (y + step) % y_n, x, zl)

    def at_row(y_step, z_step):
        return device(zh, (y + y_step) % y_n, x, (zl + z_step) % zl_n)

    other_core = {"ctx": me, "tp": zl * 2 + 1 - core}

    def remote(src, dst, send, recv, target):
        return pltpu.make_async_remote_copy(
            src_ref=src, dst_ref=dst, send_sem=send, recv_sem=recv, device_id=target, device_id_type=MESH
        )

    own_rows = pl.ds(pl.multiple_of(x * x_share + y * share, share), share)
    pairs = (
        (k_hbm, k_ref),
        (v_hbm, v_ref),
        (h_hbm, h_ref),
        (first_hbm, first_ref),
        (turn_hbm, turn_ref),
        (fwd_hbm, fwd_ref),
        (bwd_hbm, bwd_ref),
        (last_hbm, last_ref),
        (q_hbm.at[own_rows], query_in.at[place]),
        (skip_hbm, skip_ref),
        (bias_hbm, bias_ref),
    )
    loads = [pltpu.make_async_copy(src, dst, load_sem.at[n]) for n, (src, dst) in enumerate(pairs)]

    barrier = pltpu.get_barrier_semaphore()

    def greet(target):
        pl.semaphore_signal(barrier, inc=1, device_id=target, device_id_type=MESH)

    diagonal = zl == zh
    far_first = sorted(range(1, zh_n), key=lambda step: -min(step, zh_n - step))
    for step in far_first:
        greet(at_zh(step))
    for part in range(zl_n):

        @pl.when(jnp.logical_not(jnp.logical_and(diagonal, zl == part)))
        def _():
            greet(device(zl, y, x, part))

    for step in range(1, plane):
        greet(in_plane(step))
    for z_step in range(1, zl_n):
        for y_step in range(y_n):
            greet(at_row(y_step, z_step))
    greet(other_core)
    greeted = (zh_n - 1) + zl_n + (plane - 1) + (zl_n - 1) * y_n + 1

    for load in loads:
        load.start()
    for load in loads[:3]:
        load.wait()
    products = k_ref[...].astype(F32) * v_ref[...].astype(F32)
    pieces = jnp.concatenate(
        [products.reshape(blocks, GROUP, LANES), h_ref[...].reshape(blocks, GROUP, LANES)], 1
    ).astype(BF16)
    for x_at in range(x_n):
        for y_at in range(y_n):
            start = (x_at * y_n + y_at) * zh_n
            cut[y_at * x_n + x_at] = pieces[start : start + zh_n]
    pl.semaphore_wait(barrier, greeted - jnp.where(diagonal, 1, 0))

    s_copies = []
    for step in range(1, plane):
        copy = remote(
            cut.at[(place + step) % plane],
            rows_in.at[:, place],
            s_send.at[step],
            s_recv.at[step],
            in_plane(step),
        )
        copy.start()
        s_copies.append(copy)
    halves_at = [pl.ds(part * (width // 2), width // 2) for part in range(2)]
    wz_copies = [
        [
            remote(
                w_hbm.at[rows],
                w_line.at[zl, rows],
                wz_send.at[step, part],
                wz_recv.at[zl, part],
                device((zh + step) % zh_n, y, x, zh),
            )
            for part, rows in enumerate(halves_at)
        ]
        for step in range(zh_n)
    ]
    stay = [
        pltpu.make_async_copy(w_hbm.at[rows], w_line.at[zl, rows], wz_recv.at[zl, part])
        for part, rows in enumerate(halves_at)
    ]
    late = zh_n // 2
    for part in range(2):
        for step in [late] + [step for step in range(1, zh_n) if step != late]:
            if step != late or part == 0:
                wz_copies[step][part].start()

        @pl.when(diagonal)
        def _():
            stay[part].start()

        @pl.when(jnp.logical_not(diagonal))
        def _():
            wz_copies[0][part].start()

    def hand_on(part):
        for source in range(zl_n):
            block = w_line.at[source, halves_at[part]]
            pltpu.make_async_copy(block, block, wz_recv.at[source, part]).wait()
        sent = []
        for step in range(1, plane):
            columns = pl.ds(pl.multiple_of((place + step) % plane % x_n * x_share, x_share), x_share)
            copy = remote(
                w_line.at[:, halves_at[part], columns],
                weights.at[:, y, x, halves_at[part]],
                wp_send.at[step, part],
                wp_recv.at[step, part],
                in_plane(step),
            )
            copy.start()
            sent.append(copy)
        columns = pl.ds(pl.multiple_of(x * x_share, x_share), x_share)
        weights[:, y, x, halves_at[part]] = w_line[:, halves_at[part], columns]
        return sent

    rows_in[:, pl.ds(place, 1)] = cut[pl.ds(place, 1)].reshape(zh_n, 1, 2 * GROUP, LANES)
    for load in loads[3:]:
        load.wait()
    for copy in s_copies:
        copy.wait_recv()

    z_copies = []
    for step in far_first:
        copy = remote(
            rows_in.at[(zh + step) % zh_n], seq_in.at[zh], z_send.at[step], z_recv.at[step], at_zh(step)
        )
        copy.start()
        z_copies.append(copy)
    seq_in[zh] = rows_in[zh]
    q_copies = []
    for step in range(1, plane):
        target = (place + step) % plane
        rows = pl.ds(
            pl.multiple_of(target % x_n * x_share + target // x_n * share, share), share
        )
        copy = remote(
            q_hbm.at[rows], query_in.at[place], q_send.at[step], q_recv.at[step], in_plane(step)
        )
        copy.start()
        q_copies.append(copy)
    index = lax.broadcasted_iota(jnp.int32, (share, 1), 0)
    skip = column(skip_ref[...], x * x_share + y * share + index)
    wp_copies = hand_on(0)
    for copy in z_copies:
        copy.wait_recv()
    wz_copies[late][1].start()

    wide[...] = seq_in[...].reshape(blocks * 2 * GROUP, LANES).astype(F32)
    turn_re = turn_ref[0]
    turn_im = turn_ref[1]
    turn_re2 = jnp.concatenate([turn_re, turn_re], 1)
    turn_im2 = jnp.concatenate([turn_im, turn_im], 1)
    for channel in range(GROUP):
        signal = wide[pl.ds(channel, blocks, stride=2 * GROUP), :].astype(BF16)
        taps = wide[pl.ds(GROUP + channel, blocks, stride=2 * GROUP), :].astype(BF16)
        both = jnp.concatenate([signal, taps], 1)
        spread = dot(first_ref[...], jnp.concatenate([both, both], 0))
        re, im = spread[:blocks], spread[blocks:]
        turned_re = re * turn_re2 - im * turn_im2
        turned_im = re * turn_im2 + im * turn_re2
        stacked = jnp.concatenate(
            [
                jnp.concatenate([turned_re[:, :LANES], turned_im[:, :LANES]], 1),
                jnp.concatenate([turned_re[:, LANES:], turned_im[:, LANES:]], 1),
            ],
            0,
        )
        spectra = dot_split(stacked, fwd_ref)
        s_re, s_im = spectra[:blocks, :LANES], spectra[:blocks, LANES:]
        t_re, t_im = spectra[blocks:, :LANES], spectra[blocks:, LANES:]
        mixed = jnp.concatenate([s_re * t_re - s_im * t_im, s_re * t_im + s_im * t_re], 1)
        back = dot_split(mixed, bwd_ref)
        b_re, b_im = back[:, :LANES], back[:, LANES:]
        unturned = jnp.concatenate([b_re * turn_re + b_im * turn_im, b_im * turn_re - b_re * turn_im], 0)
        high, low = halves(unturned)
        conv_wide[pl.ds(channel, blocks, stride=GROUP), :] = dot(
            last_ref[...], jnp.concatenate([high, high, low], 0)
        )
    conv_out[...] = conv_wide[...].reshape(zh_n, plane, GROUP, LANES).astype(BF16)

    r_copies = []
    for step in far_first:
        copy = remote(
            conv_out.at[(zh + step) % zh_n], conv_in.at[zh], r_send.at[step], r_recv.at[step], at_zh(step)
        )
        copy.start()
        r_copies.append(copy)
    conv_in[zh] = conv_out[zh]

    wp_copies += hand_on(1)
    for copy in q_copies:
        copy.wait_recv()
    for copy in r_copies:
        copy.wait_recv()

    line_rows = pl.ds(pl.multiple_of(zl * x_share + y * share, share), share)
    offsets = sorted(range(1, x_n), key=lambda step: -min(step, x_n - step)) + [0]
    g_copies = []
    for turn, offset in enumerate(offsets):
        at = (x + offset) % x_n
        for y_at in range(y_n):
            spot = y_at * x_n + at
            long_conv = conv_in[:, pl.ds(spot, 1)].astype(F32).reshape(share, LANES)
            rows = rows_in[:, pl.ds(spot, 1)].astype(F32)[:, :, :GROUP].reshape(share, LANES)
            query = query_in[spot].astype(F32)
            gated_out[turn, y_at] = (query * (long_conv + skip * rows)).astype(BF16)
        sent = []
        for z_step in range(zl_n):
            for y_step in range(y_n):
                if z_step == 0 and y_step == 0:
                    continue
                copy = remote(
                    gated_out.at[turn, (y + y_step) % y_n],
                    gated.at[turn, line_rows],
                    g_send.at[turn, z_step, y_step],
                    g_recv.at[turn, z_step, y_step],
                    at_row(y_step, z_step),
                )
                copy.start()
                sent.append(copy)
        gated[turn, line_rows] = gated_out[turn, y]
        g_copies.append(sent)
    index = lax.broadcasted_iota(jnp.int32, (bias_ref.shape[1], 1), 0)
    bias = column(bias_ref[...], index)
    for copy in wp_copies:
        copy.wait_recv()

    half = y_n // 2

    def project(target, turn):
        blocks_at = pl.ds(target * half, half)
        block = jnp.concatenate(
            [weights[part, blocks_at].reshape(half * x_n * width, x_share) for part in range(zl_n)], 1
        )
        return dot(block, gated[turn])

    c_copies = []
    e_copies = []

    def pair_sum(turn):
        c_copies[turn].wait_recv()
        total = own_sum[turn] + pair_in[turn]
        if offsets[turn] == 0:
            return total
        sum_out[turn] = total.astype(BF16)
        copy = remote(
            sum_out.at[turn], sum_in.at[turn], e_send.at[turn], e_recv.at[turn], at_x(offsets[turn])
        )
        copy.start()
        e_copies.append(copy)

    for turn in range(x_n):
        for copy in g_copies[turn]:
            copy.wait_recv()
        pair_out[turn] = project(1 - core, turn)
        copy = remote(
            pair_out.at[turn], pair_in.at[turn], c_send.at[turn], c_recv.at[turn], other_core
        )
        copy.start()
        c_copies.append(copy)
        own_sum[turn] = project(core, turn)
        if turn:
            pair_sum(turn - 1)
    total = pair_sum(x_n - 1) + bias
    for turn in range(x_n - 1):
        e_copies[turn].wait_recv()
        total = total + sum_in[turn].astype(F32)
    out_ref[...] = total.astype(BF16)
    for copies in (s_copies, *wz_copies[1:], z_copies, q_copies, r_copies, wp_copies, c_copies, e_copies):
        for copy in copies:
            copy.wait_send()

    @pl.when(jnp.logical_not(diagonal))
    def _():
        for copy in wz_copies[0]:
            copy.wait_send()

    for sent in g_copies:
        for copy in sent:
            copy.wait_send()


def on_device(dims, query_gate, key_gate, value_input, long_filter, skip_gain, out_weight, out_bias):
    zh_n, y_n, x_n, zl_n = dims
    plane = y_n * x_n
    blocks = zh_n * plane
    channels = key_gate.shape[0]
    width = out_weight.shape[1]
    x_share = channels // x_n
    share = channels // plane
    outputs = out_bias.shape[0]
    tables = [jnp.asarray(table) for table in transform_tables(blocks)]
    dma = pltpu.SemaphoreType.DMA
    return pl.pallas_call(
        functools.partial(kernel, dims),
        out_shape=jax.ShapeDtypeStruct((outputs, LANES), BF16),
        in_specs=[pl.BlockSpec(memory_space=pltpu.HBM)] * 12,
        out_specs=pl.BlockSpec(memory_space=pltpu.VMEM),
        scratch_shapes=[
            pltpu.VMEM((channels, LANES), BF16),
            pltpu.VMEM((channels, LANES), BF16),
            pltpu.VMEM((channels, LANES), F32),
            pltpu.VMEM((1, channels), F32),
            pltpu.VMEM((1, outputs), F32),
            *[pltpu.VMEM(table.shape, table.dtype) for table in tables],
            pltpu.VMEM((plane, zh_n, 2 * GROUP, LANES), BF16),
            pltpu.VMEM((zh_n, plane, 2 * GROUP, LANES), BF16),
            pltpu.VMEM((plane, share, LANES), BF16),
            pltpu.VMEM((zh_n, plane, 2 * GROUP, LANES), BF16),
            pltpu.VMEM((blocks * 2 * GROUP, LANES), F32),
            pltpu.VMEM((blocks * GROUP, LANES), F32),
            pltpu.VMEM((zh_n, plane, GROUP, LANES), BF16),
            pltpu.VMEM((zh_n, plane, GROUP, LANES), BF16),
            pltpu.VMEM((x_n, y_n, share, LANES), BF16),
            pltpu.VMEM((x_n, channels, LANES), BF16),
            pltpu.VMEM((zl_n, width, channels), BF16),
            pltpu.VMEM((zl_n, y_n, x_n, width, x_share), BF16),
            pltpu.VMEM((x_n, outputs, LANES), F32),
            pltpu.VMEM((x_n, outputs, LANES), F32),
            pltpu.VMEM((x_n, outputs, LANES), F32),
            pltpu.VMEM((x_n, outputs, LANES), BF16),
            pltpu.VMEM((x_n, outputs, LANES), BF16),
            dma((11,)),
            dma((plane,)),
            dma((plane,)),
            dma((plane,)),
            dma((plane,)),
            dma((zh_n,)),
            dma((zh_n,)),
            dma((zh_n, 2)),
            dma((zl_n, 2)),
            dma((plane, 2)),
            dma((plane, 2)),
            dma((zh_n,)),
            dma((zh_n,)),
            dma((x_n, zl_n, y_n)),
            dma((x_n, zl_n, y_n)),
            dma((x_n,)),
            dma((x_n,)),
            dma((x_n,)),
            dma((x_n,)),
        ],
        compiler_params=pltpu.CompilerParams(
            collective_id=0, has_side_effects=True, vmem_limit_bytes=60 * 1024 * 1024
        ),
        name="hyena_mixer",
    )(
        query_gate,
        key_gate,
        value_input,
        long_filter,
        skip_gain.reshape(1, channels),
        out_weight.T,
        out_bias.reshape(1, -1),
        *tables,
    )


def solution(mesh, dims=(4, 4, 4, 4)):
    placed = (
        P("tp", "ctx"),
        P("tp", "ctx"),
        P("tp", "ctx"),
        P("tp", "ctx"),
        P("tp"),
        P("tp", "ctx"),
        P("tp"),
    )
    return jax.shard_map(
        functools.partial(on_device, dims),
        mesh=mesh,
        in_specs=placed,
        out_specs=P("tp", "ctx"),
        check_vma=False,
    )
```

```python
import functools

import jax
import jax.numpy as jnp
import numpy as np
from jax import lax
from jax.experimental import pallas as pl
from jax.experimental.pallas import tpu as pltpu
from jax.sharding import PartitionSpec as P

F32 = jnp.float32
BF16 = jnp.bfloat16
MESH = pl.DeviceIdType.MESH
LANES = 128
GROUP = 8


def split_bf16(array):
    high = array.astype(BF16)
    low = (array - np.asarray(high, np.float64)).astype(BF16)
    return np.asarray(high), np.asarray(low)


def transform_tables(blocks):
    n1 = np.arange(blocks)[:, None]
    k1 = np.arange(blocks)[None, :] + 0.5
    outer = 2.0 * np.pi * n1 * k1 / (2 * blocks)
    first = np.concatenate([np.cos(outer).T, -np.sin(outer).T], 0)
    first_hi, first_lo = split_bf16(first)
    scale = 2.0 / (2 * blocks * LANES)
    last = np.concatenate([np.cos(outer), -np.sin(outer)], 1) * scale
    last_hi, last_lo = split_bf16(last)
    lane = np.arange(LANES)
    inner = 2.0 * np.pi * (lane[:, None] * lane[None, :] % LANES) / LANES
    cos_part, sin_part = np.cos(inner), -np.sin(inner)
    forward = np.block([[cos_part, sin_part], [-sin_part, cos_part]])
    backward = np.block([[cos_part, -sin_part], [sin_part, cos_part]])
    turn = 2.0 * np.pi * k1.T * lane[None, :] / (2 * blocks * LANES)
    return (
        np.concatenate([first_hi, first_lo], 1),
        np.stack(split_bf16(forward)),
        np.stack(split_bf16(backward)),
        np.concatenate([last_hi, last_lo, last_hi], 1),
        np.stack([np.cos(turn), -np.sin(turn)]).astype(np.float32),
    )


def dot(left, right):
    return jnp.dot(left, right, preferred_element_type=F32)


def halves(value):
    high = value.astype(BF16)
    return high, (value - high.astype(F32)).astype(BF16)


def dot_split(value, table_ref):
    high, low = halves(value)
    return dot(high, table_ref[0]) + dot(low, table_ref[0]) + dot(high, table_ref[1])


def low_high(low, high, swap_low, swap_high):
    row = lax.broadcasted_iota(jnp.int32, low.shape, low.ndim - 2)
    low = pltpu.roll(low, GROUP // 2, low.ndim - 2) if swap_low else low
    high = pltpu.roll(high, GROUP // 2, high.ndim - 2) if swap_high else high
    return jnp.where(row < GROUP // 2, low, high)


def column(row, targets):
    lanes = lax.broadcasted_iota(jnp.int32, (targets.shape[0], row.shape[1]), 1)
    return jnp.sum(jnp.where(lanes == targets, row, 0.0), axis=1, keepdims=True)


def kernel(
    dims,
    q_hbm,
    k_hbm,
    v_hbm,
    h_hbm,
    skip_hbm,
    w_hbm,
    bias_hbm,
    first_hbm,
    fwd_hbm,
    bwd_hbm,
    last_hbm,
    turn_hbm,
    out_ref,
    k_ref,
    v_ref,
    h_ref,
    skip_ref,
    bias_ref,
    first_ref,
    fwd_ref,
    bwd_ref,
    last_ref,
    turn_ref,
    cut,
    rows_in,
    query_in,
    line_cut,
    seq_in,
    direct,
    long_conv,
    wide,
    conv_wide,
    conv_out,
    conv_in,
    gated_out,
    gated,
    w_line,
    weights,
    pair_out,
    pair_in,
    sum_out,
    sum_in,
    load_sem,
    s_send,
    s_recv,
    q_send,
    q_recv,
    z_send,
    z_recv,
    wz_send,
    wz_recv,
    wp_send,
    wp_recv,
    r_send,
    r_recv,
    g_send,
    g_recv,
    c_send,
    c_recv,
    e_send,
    e_recv,
):
    zh_n, y_n, x_n, zl_n = dims
    plane = y_n * x_n
    blocks = zh_n * plane
    me = lax.axis_index("ctx")
    tp = lax.axis_index("tp")
    place = me % plane
    x = me % x_n
    y = place // x_n
    zh = me // plane
    core = tp % 2
    zl = tp // 2
    channels = k_hbm.shape[0]
    x_share = channels // x_n
    share = channels // plane
    width = w_hbm.shape[0]

    def device(zh_at, y_at, x_at, zl_at, core_at=None):
        core_at = core if core_at is None else core_at
        return {"ctx": (zh_at * y_n + y_at) * x_n + x_at, "tp": zl_at * 2 + core_at}

    def in_plane(step):
        return {"ctx": zh * plane + (place + step) % plane, "tp": tp}

    def at_zh(step):
        return device((zh + step) % zh_n, y, x, zl)

    def at_x(step):
        return device(zh, y, (x + step) % x_n, zl)

    def at_y(step):
        return device(zh, (y + step) % y_n, x, zl)

    def at_row(y_step, z_step):
        return device(zh, (y + y_step) % y_n, x, (zl + z_step) % zl_n)

    other_core = {"ctx": me, "tp": zl * 2 + 1 - core}

    def remote(src, dst, send, recv, target):
        return pltpu.make_async_remote_copy(
            src_ref=src, dst_ref=dst, send_sem=send, recv_sem=recv, device_id=target, device_id_type=MESH
        )

    own_rows = pl.ds(pl.multiple_of(x * x_share + y * share, share), share)
    pairs = (
        (k_hbm, k_ref),
        (v_hbm, v_ref),
        (h_hbm, h_ref),
        (first_hbm, first_ref),
        (turn_hbm, turn_ref),
        (fwd_hbm, fwd_ref),
        (bwd_hbm, bwd_ref),
        (last_hbm, last_ref),
        (q_hbm.at[own_rows], query_in.at[place]),
        (skip_hbm, skip_ref),
        (bias_hbm, bias_ref),
    )
    loads = [pltpu.make_async_copy(src, dst, load_sem.at[n]) for n, (src, dst) in enumerate(pairs)]

    barrier = pltpu.get_barrier_semaphore()

    def greet(target):
        pl.semaphore_signal(barrier, inc=1, device_id=target, device_id_type=MESH)

    diagonal = zl == zh
    far_first = sorted(range(1, zh_n), key=lambda step: -min(step, zh_n - step))
    for step in far_first:
        greet(at_zh(step))
    for part in range(zl_n):

        @pl.when(jnp.logical_not(jnp.logical_and(diagonal, zl == part)))
        def _():
            greet(device(zl, y, x, part))

    for step in range(1, plane):
        greet(in_plane(step))
    for z_step in range(1, zl_n):
        for y_step in range(y_n):
            greet(at_row(y_step, z_step))
    for step in range(x_n):
        greet(device(zh, y, (x + step) % x_n, zl, 1 - core))
    greeted = (zh_n - 1) + zl_n + (plane - 1) + (zl_n - 1) * y_n + x_n

    for load in loads:
        load.start()
    for load in loads[:3]:
        load.wait()
    products = (k_ref[...].astype(F32) * v_ref[...].astype(F32)).reshape(blocks, GROUP, LANES)
    taps = h_ref[...].reshape(blocks, GROUP, LANES)
    pieces = (low_high(products, taps, False, True), low_high(products, taps, True, False))
    for part in range(2):
        packed = pieces[part].reshape(blocks // 2, 2 * GROUP, LANES).astype(BF16)
        for x_at in range(x_n):
            for y_at in range(y_n):
                start = (x_at * y_n + y_at) * zh_n // 2
                cut[part, y_at * x_n + x_at] = packed[start : start + zh_n // 2]
    pl.semaphore_wait(barrier, greeted - jnp.where(diagonal, 1, 0))

    s_copies = []
    for part in range(2):
        sent = []
        for step in range(1, plane):
            copy = remote(
                cut.at[part, (place + step) % plane],
                rows_in.at[part, :, place],
                s_send.at[step, part],
                s_recv.at[step, part],
                in_plane(step),
            )
            copy.start()
            sent.append(copy)
        s_copies.append(sent)
    halves_at = [pl.ds(part * (width // 2), width // 2) for part in range(2)]
    wz_copies = [
        [
            remote(
                w_hbm.at[rows],
                w_line.at[zl, rows],
                wz_send.at[step, part],
                wz_recv.at[zl, part],
                device((zh + step) % zh_n, y, x, zh),
            )
            for part, rows in enumerate(halves_at)
        ]
        for step in range(zh_n)
    ]
    stay = [
        pltpu.make_async_copy(w_hbm.at[rows], w_line.at[zl, rows], wz_recv.at[zl, part])
        for part, rows in enumerate(halves_at)
    ]
    late = zh_n // 2

    def send_far(part):
        wz_copies[late][part].start()

    def send_near(part):
        for step in range(1, zh_n):
            if step != late:
                wz_copies[step][part].start()

        @pl.when(diagonal)
        def _():
            stay[part].start()

        @pl.when(jnp.logical_not(diagonal))
        def _():
            wz_copies[0][part].start()

    send_far(0)
    send_near(0)

    def hand_on(part):
        for source in range(zl_n):
            block = w_line.at[source, halves_at[part]]
            pltpu.make_async_copy(block, block, wz_recv.at[source, part]).wait()
        sent = []
        for step in range(1, plane):
            columns = pl.ds(pl.multiple_of((place + step) % plane % x_n * x_share, x_share), x_share)
            copy = remote(
                w_line.at[:, halves_at[part], columns],
                weights.at[:, y, x, halves_at[part]],
                wp_send.at[step, part],
                wp_recv.at[step, part],
                in_plane(step),
            )
            copy.start()
            sent.append(copy)
        columns = pl.ds(pl.multiple_of(x * x_share, x_share), x_share)
        weights[:, y, x, halves_at[part]] = w_line[:, halves_at[part], columns]
        return sent

    for part in range(2):
        rows_in[part, :, pl.ds(place, 1)] = cut[part, pl.ds(place, 1)].reshape(
            zh_n // 2, 1, 2 * GROUP, LANES
        )
    for load in loads[3:]:
        load.wait()

    index = lax.broadcasted_iota(jnp.int32, (share, 1), 0)
    skip = column(skip_ref[...], x * x_share + y * share + index).reshape(zh_n, 1, GROUP, 1)
    z_copies = []
    arrived = []
    for part in range(2):
        for copy in s_copies[part]:
            copy.wait_recv()
        value = rows_in[part].astype(F32).reshape(zh_n // 2, plane, 2, GROUP, LANES)
        arrived.append(value)
        for zh_at in range(zh_n):
            line_cut[part, zh_at] = (
                value[zh_at // 2, :, zh_at % 2].reshape(plane // 2, 2 * GROUP, LANES).astype(BF16)
            )
        sent = []
        for step in far_first:
            copy = remote(
                line_cut.at[part, (zh + step) % zh_n],
                seq_in.at[part, zh],
                z_send.at[step, part],
                z_recv.at[step, part],
                at_zh(step),
            )
            copy.start()
            sent.append(copy)
        seq_in[part, pl.ds(zh, 1)] = line_cut[part, pl.ds(zh, 1)]
        z_copies.append(sent)
    for zh_at in range(zh_n):
        first, second = (value[zh_at // 2, :, zh_at % 2] for value in arrived)
        direct[:, zh_at] = skip[zh_at] * low_high(first, second, False, True)
    q_copies = []
    for step in range(1, plane):
        target = (place + step) % plane
        rows = pl.ds(
            pl.multiple_of(target % x_n * x_share + target // x_n * share, share), share
        )
        copy = remote(
            q_hbm.at[rows], query_in.at[place], q_send.at[step], q_recv.at[step], in_plane(step)
        )
        copy.start()
        q_copies.append(copy)
    wp_copies = hand_on(0)
    turn_re = turn_ref[0]
    turn_im = turn_ref[1]
    turn_re2 = jnp.concatenate([turn_re, turn_re], 1)
    turn_im2 = jnp.concatenate([turn_im, turn_im], 1)
    r_copies = []
    for part in range(2):
        for copy in z_copies[part]:
            copy.wait_recv()
        if part:
            send_far(1)
        wide[part] = seq_in[part].astype(F32).reshape(blocks * GROUP, LANES)
        for channel in range(GROUP // 2):
            signal = wide[part, pl.ds(channel, blocks, stride=GROUP), :].astype(BF16)
            taps = wide[part, pl.ds(GROUP // 2 + channel, blocks, stride=GROUP), :].astype(BF16)
            both = jnp.concatenate([signal, taps], 1)
            spread = dot(first_ref[...], jnp.concatenate([both, both], 0))
            re, im = spread[:blocks], spread[blocks:]
            turned_re = re * turn_re2 - im * turn_im2
            turned_im = re * turn_im2 + im * turn_re2
            stacked = jnp.concatenate(
                [
                    jnp.concatenate([turned_re[:, :LANES], turned_im[:, :LANES]], 1),
                    jnp.concatenate([turned_re[:, LANES:], turned_im[:, LANES:]], 1),
                ],
                0,
            )
            spectra = dot_split(stacked, fwd_ref)
            s_re, s_im = spectra[:blocks, :LANES], spectra[:blocks, LANES:]
            t_re, t_im = spectra[blocks:, :LANES], spectra[blocks:, LANES:]
            mixed = jnp.concatenate([s_re * t_re - s_im * t_im, s_re * t_im + s_im * t_re], 1)
            back = dot_split(mixed, bwd_ref)
            b_re, b_im = back[:, :LANES], back[:, LANES:]
            unturned = jnp.concatenate([b_re * turn_re + b_im * turn_im, b_im * turn_re - b_re * turn_im], 0)
            high, low = halves(unturned)
            conv_wide[part, pl.ds(channel, blocks, stride=GROUP // 2), :] = dot(
                last_ref[...], jnp.concatenate([high, high, low], 0)
            )
        conv_out[part] = conv_wide[part].reshape(zh_n, plane * GROUP // 2, LANES).astype(BF16)
        for step in far_first:
            copy = remote(
                conv_out.at[part, (zh + step) % zh_n],
                conv_in.at[part, zh],
                r_send.at[step, part],
                r_recv.at[step, part],
                at_zh(step),
            )
            copy.start()
            r_copies.append(copy)
        conv_in[part, pl.ds(zh, 1)] = conv_out[part, pl.ds(zh, 1)]
    send_near(1)
    wp_copies += hand_on(1)
    for copy in q_copies:
        copy.wait_recv()
    for copy in r_copies:
        copy.wait_recv()
    first, second = (
        conv_in[part].astype(F32).reshape(zh_n, plane // 2, GROUP, LANES) for part in range(2)
    )
    for spot in range(plane):
        odd = spot % 2 == 1
        long_conv[spot] = direct[spot] + low_high(first[:, spot // 2], second[:, spot // 2], odd, not odd)

    line_rows = pl.ds(pl.multiple_of(zl * x_share + y * share, share), share)
    offsets = sorted(range(1, x_n), key=lambda step: -min(step, x_n - step)) + [0]
    g_copies = []
    for turn, offset in enumerate(offsets):
        at = (x + offset) % x_n
        for y_at in range(y_n):
            spot = y_at * x_n + at
            query = query_in[spot].astype(F32)
            gated_out[turn, y_at] = (query * long_conv[spot].reshape(share, LANES)).astype(BF16)
        sent = []
        for z_step in range(zl_n):
            for y_step in range(y_n):
                if z_step == 0 and y_step == 0:
                    continue
                copy = remote(
                    gated_out.at[turn, (y + y_step) % y_n],
                    gated.at[turn, line_rows],
                    g_send.at[turn, z_step, y_step],
                    g_recv.at[turn, z_step, y_step],
                    at_row(y_step, z_step),
                )
                copy.start()
                sent.append(copy)
        gated[turn, line_rows] = gated_out[turn, y]
        g_copies.append(sent)
    index = lax.broadcasted_iota(jnp.int32, (bias_ref.shape[1], 1), 0)
    bias = column(bias_ref[...], index)
    for copy in wp_copies:
        copy.wait_recv()

    half = y_n // 2

    def project(target, turn):
        blocks_at = pl.ds(target * half, half)
        block = jnp.concatenate(
            [weights[part, blocks_at].reshape(half * x_n * width, x_share) for part in range(zl_n)], 1
        )
        return dot(block, gated[turn])

    e_copies = []
    for turn in range(x_n - 1):
        for copy in g_copies[turn]:
            copy.wait_recv()
        for side in range(2):
            sum_out[turn, side] = project((core + side) % 2, turn).astype(BF16)
            copy = remote(
                sum_out.at[turn, side],
                sum_in.at[turn, side],
                e_send.at[turn, side],
                e_recv.at[turn, side],
                device(zh, y, (x + offsets[turn]) % x_n, zl, (core + side) % 2),
            )
            copy.start()
            e_copies.append(copy)
    for copy in g_copies[x_n - 1]:
        copy.wait_recv()
    pair_out[...] = project(1 - core, x_n - 1)
    pair_copy = remote(pair_out, pair_in, c_send, c_recv, other_core)
    pair_copy.start()
    total = project(core, x_n - 1) + bias
    for turn in range(x_n - 1):
        for side in range(2):
            e_copies[2 * turn + side].wait_recv()
            total = total + sum_in[turn, side].astype(F32)
    pair_copy.wait_recv()
    total = total + pair_in[...]
    out_ref[...] = total.astype(BF16)
    for copies in (*s_copies, *wz_copies[1:], *z_copies, q_copies, r_copies, wp_copies, [pair_copy], e_copies):
        for copy in copies:
            copy.wait_send()

    @pl.when(jnp.logical_not(diagonal))
    def _():
        for copy in wz_copies[0]:
            copy.wait_send()

    for sent in g_copies:
        for copy in sent:
            copy.wait_send()


def on_device(dims, query_gate, key_gate, value_input, long_filter, skip_gain, out_weight, out_bias):
    zh_n, y_n, x_n, zl_n = dims
    plane = y_n * x_n
    blocks = zh_n * plane
    channels = key_gate.shape[0]
    width = out_weight.shape[1]
    x_share = channels // x_n
    share = channels // plane
    outputs = out_bias.shape[0]
    tables = [jnp.asarray(table) for table in transform_tables(blocks)]
    dma = pltpu.SemaphoreType.DMA
    return pl.pallas_call(
        functools.partial(kernel, dims),
        out_shape=jax.ShapeDtypeStruct((outputs, LANES), BF16),
        in_specs=[pl.BlockSpec(memory_space=pltpu.HBM)] * 12,
        out_specs=pl.BlockSpec(memory_space=pltpu.VMEM),
        scratch_shapes=[
            pltpu.VMEM((channels, LANES), BF16),
            pltpu.VMEM((channels, LANES), BF16),
            pltpu.VMEM((channels, LANES), F32),
            pltpu.VMEM((1, channels), F32),
            pltpu.VMEM((1, outputs), F32),
            *[pltpu.VMEM(table.shape, table.dtype) for table in tables],
            pltpu.VMEM((2, plane, zh_n // 2, 2 * GROUP, LANES), BF16),
            pltpu.VMEM((2, zh_n // 2, plane, 2 * GROUP, LANES), BF16),
            pltpu.VMEM((plane, share, LANES), BF16),
            pltpu.VMEM((2, zh_n, plane // 2, 2 * GROUP, LANES), BF16),
            pltpu.VMEM((2, zh_n, plane // 2, 2 * GROUP, LANES), BF16),
            pltpu.VMEM((plane, zh_n, GROUP, LANES), F32),
            pltpu.VMEM((plane, zh_n, GROUP, LANES), F32),
            pltpu.VMEM((2, blocks * GROUP, LANES), F32),
            pltpu.VMEM((2, blocks * GROUP // 2, LANES), F32),
            pltpu.VMEM((2, zh_n, plane * GROUP // 2, LANES), BF16),
            pltpu.VMEM((2, zh_n, plane * GROUP // 2, LANES), BF16),
            pltpu.VMEM((x_n, y_n, share, LANES), BF16),
            pltpu.VMEM((x_n, channels, LANES), BF16),
            pltpu.VMEM((zl_n, width, channels), BF16),
            pltpu.VMEM((zl_n, y_n, x_n, width, x_share), BF16),
            pltpu.VMEM((outputs, LANES), F32),
            pltpu.VMEM((outputs, LANES), F32),
            pltpu.VMEM((x_n - 1, 2, outputs, LANES), BF16),
            pltpu.VMEM((x_n - 1, 2, outputs, LANES), BF16),
            dma((11,)),
            dma((plane, 2)),
            dma((plane, 2)),
            dma((plane,)),
            dma((plane,)),
            dma((zh_n, 2)),
            dma((zh_n, 2)),
            dma((zh_n, 2)),
            dma((zl_n, 2)),
            dma((plane, 2)),
            dma((plane, 2)),
            dma((zh_n, 2)),
            dma((zh_n, 2)),
            dma((x_n, zl_n, y_n)),
            dma((x_n, zl_n, y_n)),
            dma,
            dma,
            dma((x_n - 1, 2)),
            dma((x_n - 1, 2)),
        ],
        compiler_params=pltpu.CompilerParams(
            collective_id=0, has_side_effects=True, vmem_limit_bytes=60 * 1024 * 1024
        ),
        name="hyena_mixer",
    )(
        query_gate,
        key_gate,
        value_input,
        long_filter,
        skip_gain.reshape(1, channels),
        out_weight.T,
        out_bias.reshape(1, -1),
        *tables,
    )


def solution(mesh, dims=(4, 4, 4, 4)):
    placed = (
        P("tp", "ctx"),
        P("tp", "ctx"),
        P("tp", "ctx"),
        P("tp", "ctx"),
        P("tp"),
        P("tp", "ctx"),
        P("tp"),
    )
    return jax.shard_map(
        functools.partial(on_device, dims),
        mesh=mesh,
        in_specs=placed,
        out_specs=P("tp", "ctx"),
        check_vma=False,
    )
```

```python
import functools

import jax
import jax.numpy as jnp
import numpy as np
from jax import lax
from jax.experimental import pallas as pl
from jax.experimental.pallas import tpu as pltpu
from jax.sharding import PartitionSpec as P

F32 = jnp.float32
BF16 = jnp.bfloat16
MESH = pl.DeviceIdType.MESH
LANES = 128
GROUP = 8


def split_bf16(array):
    high = array.astype(BF16)
    low = (array - np.asarray(high, np.float64)).astype(BF16)
    return np.asarray(high), np.asarray(low)


def transform_tables(blocks):
    n1 = np.arange(blocks)[:, None]
    k1 = np.arange(blocks)[None, :] + 0.5
    outer = 2.0 * np.pi * n1 * k1 / (2 * blocks)
    first = np.concatenate([np.cos(outer).T, -np.sin(outer).T], 0)
    first_hi, first_lo = split_bf16(first)
    scale = 2.0 / (2 * blocks * LANES)
    last = np.concatenate([np.cos(outer), -np.sin(outer)], 1) * scale
    last_hi, last_lo = split_bf16(last)
    lane = np.arange(LANES)
    inner = 2.0 * np.pi * (lane[:, None] * lane[None, :] % LANES) / LANES
    cos_part, sin_part = np.cos(inner), -np.sin(inner)
    forward = np.block([[cos_part, sin_part], [-sin_part, cos_part]])
    backward = np.block([[cos_part, -sin_part], [sin_part, cos_part]])
    turn = 2.0 * np.pi * k1.T * lane[None, :] / (2 * blocks * LANES)
    return (
        np.concatenate([first_hi, first_lo], 1),
        np.stack(split_bf16(forward)),
        np.stack(split_bf16(backward)),
        np.concatenate([last_hi, last_lo, last_hi], 1),
        np.stack([np.cos(turn), -np.sin(turn)]).astype(np.float32),
    )


def dot(left, right):
    return jnp.dot(left, right, preferred_element_type=F32)


def halves(value):
    high = value.astype(BF16)
    return high, (value - high.astype(F32)).astype(BF16)


def dot_split(value, table_ref):
    high, low = halves(value)
    return dot(high, table_ref[0]) + dot(low, table_ref[0]) + dot(high, table_ref[1])


def low_high(low, high, swap_low, swap_high):
    row = lax.broadcasted_iota(jnp.int32, low.shape, low.ndim - 2)
    low = pltpu.roll(low, GROUP // 2, low.ndim - 2) if swap_low else low
    high = pltpu.roll(high, GROUP // 2, high.ndim - 2) if swap_high else high
    return jnp.where(row < GROUP // 2, low, high)


def column(row, targets):
    lanes = lax.broadcasted_iota(jnp.int32, (targets.shape[0], row.shape[1]), 1)
    return jnp.sum(jnp.where(lanes == targets, row, 0.0), axis=1, keepdims=True)


def kernel(
    dims,
    q_hbm,
    k_hbm,
    v_hbm,
    h_hbm,
    skip_hbm,
    w_hbm,
    bias_hbm,
    first_hbm,
    fwd_hbm,
    bwd_hbm,
    last_hbm,
    turn_hbm,
    out_ref,
    k_ref,
    v_ref,
    h_ref,
    skip_ref,
    bias_ref,
    first_ref,
    fwd_ref,
    bwd_ref,
    last_ref,
    turn_ref,
    cut,
    rows_in,
    query_in,
    line_cut,
    seq_in,
    direct,
    long_conv,
    wide,
    conv_wide,
    conv_out,
    conv_in,
    gated_out,
    gated,
    w_line,
    weights,
    pair_out,
    pair_in,
    sum_out,
    sum_in,
    load_sem,
    s_send,
    s_recv,
    q_send,
    q_recv,
    z_send,
    z_recv,
    wz_send,
    wf_send,
    w_recv,
    wp_send,
    wp_recv,
    r_send,
    r_recv,
    g_send,
    g_recv,
    c_send,
    c_recv,
    e_send,
    e_recv,
):
    zh_n, y_n, x_n, zl_n = dims
    plane = y_n * x_n
    blocks = zh_n * plane
    me = lax.axis_index("ctx")
    tp = lax.axis_index("tp")
    place = me % plane
    x = me % x_n
    y = place // x_n
    zh = me // plane
    core = tp % 2
    zl = tp // 2
    channels = k_hbm.shape[0]
    x_share = channels // x_n
    share = channels // plane
    width = w_hbm.shape[0]

    def device(zh_at, y_at, x_at, zl_at, core_at=None):
        core_at = core if core_at is None else core_at
        return {"ctx": (zh_at * y_n + y_at) * x_n + x_at, "tp": zl_at * 2 + core_at}

    def in_plane(step):
        return {"ctx": zh * plane + (place + step) % plane, "tp": tp}

    def at_zh(step):
        return device((zh + step) % zh_n, y, x, zl)

    def at_x(step):
        return device(zh, y, (x + step) % x_n, zl)

    def at_y(step):
        return device(zh, (y + step) % y_n, x, zl)

    def at_row(y_step, z_step):
        return device(zh, (y + y_step) % y_n, x, (zl + z_step) % zl_n)

    other_core = {"ctx": me, "tp": zl * 2 + 1 - core}

    def remote(src, dst, send, recv, target):
        return pltpu.make_async_remote_copy(
            src_ref=src, dst_ref=dst, send_sem=send, recv_sem=recv, device_id=target, device_id_type=MESH
        )

    own_rows = pl.ds(pl.multiple_of(x * x_share + y * share, share), share)
    pairs = (
        (k_hbm, k_ref),
        (v_hbm, v_ref),
        (h_hbm, h_ref),
        (first_hbm, first_ref),
        (turn_hbm, turn_ref),
        (fwd_hbm, fwd_ref),
        (bwd_hbm, bwd_ref),
        (last_hbm, last_ref),
        (q_hbm.at[own_rows], query_in.at[place]),
        (skip_hbm, skip_ref),
        (bias_hbm, bias_ref),
    )
    loads = [pltpu.make_async_copy(src, dst, load_sem.at[n]) for n, (src, dst) in enumerate(pairs)]

    barrier = pltpu.get_barrier_semaphore()

    def greet(target):
        pl.semaphore_signal(barrier, inc=1, device_id=target, device_id_type=MESH)

    diagonal = zl == zh
    apart = (zh - zl + zh_n) % zh_n
    last = zh_n - 1
    far_first = sorted(range(1, zh_n), key=lambda step: -min(step, zh_n - step))

    def direct_piece(part):
        above = jnp.logical_and(apart == 1, zl <= part)
        below = jnp.logical_and(apart == last, zl >= part)
        return jnp.logical_or(apart == 0, jnp.logical_or(above, below))

    for step in far_first:
        greet(at_zh(step))
    for part in range(zl_n):

        @pl.when(jnp.logical_and(zl != part, direct_piece(part)))
        def _():
            greet(device(zl, y, x, part))

    for step in range(1, plane):
        greet(in_plane(step))
    for z_step in range(1, zl_n):
        for y_step in range(y_n):
            greet(at_row(y_step, z_step))
    greet(other_core)
    greeted = (zh_n - 1) + (plane - 1) + (zl_n - 1) * y_n + 1

    for load in loads:
        load.start()
    for load in loads[:3]:
        load.wait()
    products = (k_ref[...].astype(F32) * v_ref[...].astype(F32)).reshape(blocks, GROUP, LANES)
    taps = h_ref[...].reshape(blocks, GROUP, LANES)
    pieces = (low_high(products, taps, False, True), low_high(products, taps, True, False))
    for part in range(2):
        packed = pieces[part].reshape(blocks // 2, 2 * GROUP, LANES).astype(BF16)
        for x_at in range(x_n):
            for y_at in range(y_n):
                start = (x_at * y_n + y_at) * zh_n // 2
                cut[part, y_at * x_n + x_at] = packed[start : start + zh_n // 2]
    pl.semaphore_wait(barrier, greeted + jnp.where(diagonal, 0, 2))

    s_copies = []
    for part in range(2):
        sent = []
        for step in range(1, plane):
            copy = remote(
                cut.at[part, (place + step) % plane],
                rows_in.at[part, :, place],
                s_send.at[step, part],
                s_recv.at[step, part],
                in_plane(step),
            )
            copy.start()
            sent.append(copy)
        s_copies.append(sent)
    def own_piece(slot, step):
        return remote(
            w_hbm, w_line.at[zl], wz_send.at[slot], w_recv.at[zl], device((zh + step) % zh_n, y, x, zh)
        )

    source_copies = (
        (zl >= zh, own_piece(0, 1)),
        (zl <= zh, own_piece(1, last)),
        (jnp.logical_not(diagonal), own_piece(2, 0)),
    )
    stay = pltpu.make_async_copy(w_hbm, w_line.at[zl], w_recv.at[zl])
    for when, copy in source_copies:

        @pl.when(when)
        def _():
            copy.start()

    @pl.when(diagonal)
    def _():
        stay.start()

    def relay(part, step, slot, rows=slice(None)):
        piece = w_line.at[part, rows]
        return remote(piece, piece, wf_send.at[slot[0], slot[1]], w_recv.at[part], at_zh(step))

    relay_copies = []
    for part in range(zl_n):
        inner = jnp.logical_and(apart == 0, zl != part)
        for up in range(2):
            step = 1 if up else last
            side = (zl > part) if up else (zl < part)
            relay_copies.append((jnp.logical_and(inner, side), relay(part, step, (part, up))))
        for up in range(2):
            step = 1 if up else last
            outer = apart == (1 if up else last)
            side = (zl < part) if up else (zl > part)
            rows = pl.ds(0, width // 2) if up else pl.ds(width // 2, width // 2)
            relay_copies.append((jnp.logical_and(outer, side), relay(part, step, (part, up))))
            relay_copies.append(
                (jnp.logical_and(outer, zl == part), relay(part, step, (part, up), rows))
            )

    wp_copies = []
    for part in range(zl_n):
        sent = []
        for step in range(1, plane):
            columns = pl.ds(pl.multiple_of((place + step) % plane % x_n * x_share, x_share), x_share)
            sent.append(
                remote(
                    w_line.at[part, :, columns],
                    weights.at[part, y, x],
                    wp_send.at[part, step],
                    wp_recv.at[part, step],
                    in_plane(step),
                )
            )
        wp_copies.append(sent)

    def piece_in(part):
        pltpu.make_async_copy(w_line.at[part], w_line.at[part], w_recv.at[part]).wait()

    def hand_on(part):
        for copy in wp_copies[part]:
            copy.start()
        columns = pl.ds(pl.multiple_of(x * x_share, x_share), x_share)
        weights[part, y, x] = w_line[part, :, columns]

    for part in range(2):
        rows_in[part, :, pl.ds(place, 1)] = cut[part, pl.ds(place, 1)].reshape(
            zh_n // 2, 1, 2 * GROUP, LANES
        )
    for load in loads[3:]:
        load.wait()

    index = lax.broadcasted_iota(jnp.int32, (share, 1), 0)
    skip = column(skip_ref[...], x * x_share + y * share + index).reshape(zh_n, 1, GROUP, 1)
    z_copies = []
    arrived = []
    for part in range(2):
        for copy in s_copies[part]:
            copy.wait_recv()
        value = rows_in[part].astype(F32).reshape(zh_n // 2, plane, 2, GROUP, LANES)
        arrived.append(value)
        for zh_at in range(zh_n):
            line_cut[part, zh_at] = (
                value[zh_at // 2, :, zh_at % 2].reshape(plane // 2, 2 * GROUP, LANES).astype(BF16)
            )
        sent = []
        for step in far_first:
            copy = remote(
                line_cut.at[part, (zh + step) % zh_n],
                seq_in.at[part, zh],
                z_send.at[step, part],
                z_recv.at[step, part],
                at_zh(step),
            )
            copy.start()
            sent.append(copy)
        seq_in[part, pl.ds(zh, 1)] = line_cut[part, pl.ds(zh, 1)]
        z_copies.append(sent)
    for zh_at in range(zh_n):
        first, second = (value[zh_at // 2, :, zh_at % 2] for value in arrived)
        direct[:, zh_at] = skip[zh_at] * low_high(first, second, False, True)
    q_copies = []
    for step in range(1, plane):
        target = (place + step) % plane
        rows = pl.ds(
            pl.multiple_of(target % x_n * x_share + target // x_n * share, share), share
        )
        copy = remote(
            q_hbm.at[rows], query_in.at[place], q_send.at[step], q_recv.at[step], in_plane(step)
        )
        copy.start()
        q_copies.append(copy)

    for part in range(zl_n):

        @pl.when(direct_piece(part))
        def _():
            piece_in(part)

    for when, copy in relay_copies:

        @pl.when(when)
        def _():
            copy.start()

    for part in range(zl_n):

        @pl.when(direct_piece(part))
        def _():
            hand_on(part)

    turn_re = turn_ref[0]
    turn_im = turn_ref[1]
    turn_re2 = jnp.concatenate([turn_re, turn_re], 1)
    turn_im2 = jnp.concatenate([turn_im, turn_im], 1)
    r_copies = []
    for part in range(2):
        for copy in z_copies[part]:
            copy.wait_recv()
        wide[part] = seq_in[part].astype(F32).reshape(blocks * GROUP, LANES)
        group = range(GROUP // 2)
        spread = []
        for channel in group:
            signal = wide[part, pl.ds(channel, blocks, stride=GROUP), :].astype(BF16)
            taps = wide[part, pl.ds(GROUP // 2 + channel, blocks, stride=GROUP), :].astype(BF16)
            both = jnp.concatenate([signal, taps], 1)
            spread.append(dot(first_ref[...], jnp.concatenate([both, both], 0)))
        stacked = []
        for value in spread:
            re, im = value[:blocks], value[blocks:]
            turned_re = re * turn_re2 - im * turn_im2
            turned_im = re * turn_im2 + im * turn_re2
            stacked.append(jnp.concatenate([turned_re[:, :LANES], turned_im[:, :LANES]], 1))
            stacked.append(jnp.concatenate([turned_re[:, LANES:], turned_im[:, LANES:]], 1))
        spectra = dot_split(jnp.concatenate(stacked, 0), fwd_ref)
        mixed = []
        for channel in group:
            one = spectra[2 * channel * blocks : (2 * channel + 1) * blocks]
            two = spectra[(2 * channel + 1) * blocks : (2 * channel + 2) * blocks]
            s_re, s_im, t_re, t_im = one[:, :LANES], one[:, LANES:], two[:, :LANES], two[:, LANES:]
            mixed.append(jnp.concatenate([s_re * t_re - s_im * t_im, s_re * t_im + s_im * t_re], 1))
        back = dot_split(jnp.concatenate(mixed, 0), bwd_ref)
        unturned = []
        for channel in group:
            one = back[channel * blocks : (channel + 1) * blocks]
            b_re, b_im = one[:, :LANES], one[:, LANES:]
            unturned.append(
                jnp.concatenate([b_re * turn_re + b_im * turn_im, b_im * turn_re - b_re * turn_im], 0)
            )
        for channel in range(0, GROUP // 2, 2):
            high, low = halves(jnp.concatenate(unturned[channel : channel + 2], 1))
            result = dot(last_ref[...], jnp.concatenate([high, high, low], 0))
            conv_wide[part, pl.ds(channel, blocks, stride=GROUP // 2), :] = result[:, :LANES]
            conv_wide[part, pl.ds(channel + 1, blocks, stride=GROUP // 2), :] = result[:, LANES:]
        conv_out[part] = conv_wide[part].reshape(zh_n, plane * GROUP // 2, LANES).astype(BF16)
        for step in far_first:
            copy = remote(
                conv_out.at[part, (zh + step) % zh_n],
                conv_in.at[part, zh],
                r_send.at[step, part],
                r_recv.at[step, part],
                at_zh(step),
            )
            copy.start()
            r_copies.append(copy)
        conv_in[part, pl.ds(zh, 1)] = conv_out[part, pl.ds(zh, 1)]

    for part in range(zl_n):

        @pl.when(jnp.logical_not(direct_piece(part)))
        def _():
            piece_in(part)
            hand_on(part)

    for copy in q_copies:
        copy.wait_recv()
    for copy in r_copies:
        copy.wait_recv()
    first, second = (
        conv_in[part].astype(F32).reshape(zh_n, plane // 2, GROUP, LANES) for part in range(2)
    )
    for spot in range(plane):
        odd = spot % 2 == 1
        long_conv[spot] = direct[spot] + low_high(first[:, spot // 2], second[:, spot // 2], odd, not odd)

    line_rows = pl.ds(pl.multiple_of(zl * x_share + y * share, share), share)
    offsets = sorted(range(1, x_n), key=lambda step: -min(step, x_n - step)) + [0]
    g_copies = []
    for turn, offset in enumerate(offsets):
        at = (x + offset) % x_n
        for y_at in range(y_n):
            spot = y_at * x_n + at
            query = query_in[spot].astype(F32)
            gated_out[turn, y_at] = (query * long_conv[spot].reshape(share, LANES)).astype(BF16)
        sent = []
        for z_step in range(zl_n):
            for y_step in range(y_n):
                if z_step == 0 and y_step == 0:
                    continue
                copy = remote(
                    gated_out.at[turn, (y + y_step) % y_n],
                    gated.at[turn, line_rows],
                    g_send.at[turn, z_step, y_step],
                    g_recv.at[turn, z_step, y_step],
                    at_row(y_step, z_step),
                )
                copy.start()
                sent.append(copy)
        gated[turn, line_rows] = gated_out[turn, y]
        g_copies.append(sent)
    index = lax.broadcasted_iota(jnp.int32, (bias_ref.shape[1], 1), 0)
    bias = column(bias_ref[...], index)
    for sent in wp_copies:
        for copy in sent:
            copy.wait_recv()

    half = y_n // 2

    def project(target, turn):
        blocks_at = pl.ds(target * half, half)
        block = jnp.concatenate(
            [weights[part, blocks_at].reshape(half * x_n * width, x_share) for part in range(zl_n)], 1
        )
        return dot(block, gated[turn])

    c_copies = []
    e_copies = []
    for turn in range(x_n):
        for copy in g_copies[turn]:
            copy.wait_recv()
        pair_out[turn] = project(1 - core, turn)
        pair_copy = remote(
            pair_out.at[turn], pair_in.at[turn], c_send.at[turn], c_recv.at[turn], other_core
        )
        pair_copy.start()
        c_copies.append(pair_copy)
        total = project(core, turn)
        pair_copy.wait_recv()
        total = total + pair_in[turn]
        if turn < x_n - 1:
            sum_out[turn] = total.astype(BF16)
            copy = remote(
                sum_out.at[turn], sum_in.at[turn], e_send.at[turn], e_recv.at[turn], at_x(offsets[turn])
            )
            copy.start()
            e_copies.append(copy)
    total = total + bias
    for turn in range(x_n - 1):
        e_copies[turn].wait_recv()
        total = total + sum_in[turn].astype(F32)
    out_ref[...] = total.astype(BF16)
    for copies in (*s_copies, *z_copies, q_copies, r_copies, *wp_copies, c_copies, e_copies):
        for copy in copies:
            copy.wait_send()

    for when, copy in source_copies + tuple(relay_copies):

        @pl.when(when)
        def _():
            copy.wait_send()

    for sent in g_copies:
        for copy in sent:
            copy.wait_send()


def on_device(dims, query_gate, key_gate, value_input, long_filter, skip_gain, out_weight, out_bias):
    zh_n, y_n, x_n, zl_n = dims
    plane = y_n * x_n
    blocks = zh_n * plane
    channels = key_gate.shape[0]
    width = out_weight.shape[1]
    x_share = channels // x_n
    share = channels // plane
    outputs = out_bias.shape[0]
    tables = [jnp.asarray(table) for table in transform_tables(blocks)]
    dma = pltpu.SemaphoreType.DMA
    return pl.pallas_call(
        functools.partial(kernel, dims),
        out_shape=jax.ShapeDtypeStruct((outputs, LANES), BF16),
        in_specs=[pl.BlockSpec(memory_space=pltpu.HBM)] * 12,
        out_specs=pl.BlockSpec(memory_space=pltpu.VMEM),
        scratch_shapes=[
            pltpu.VMEM((channels, LANES), BF16),
            pltpu.VMEM((channels, LANES), BF16),
            pltpu.VMEM((channels, LANES), F32),
            pltpu.VMEM((1, channels), F32),
            pltpu.VMEM((1, outputs), F32),
            *[pltpu.VMEM(table.shape, table.dtype) for table in tables],
            pltpu.VMEM((2, plane, zh_n // 2, 2 * GROUP, LANES), BF16),
            pltpu.VMEM((2, zh_n // 2, plane, 2 * GROUP, LANES), BF16),
            pltpu.VMEM((plane, share, LANES), BF16),
            pltpu.VMEM((2, zh_n, plane // 2, 2 * GROUP, LANES), BF16),
            pltpu.VMEM((2, zh_n, plane // 2, 2 * GROUP, LANES), BF16),
            pltpu.VMEM((plane, zh_n, GROUP, LANES), F32),
            pltpu.VMEM((plane, zh_n, GROUP, LANES), F32),
            pltpu.VMEM((2, blocks * GROUP, LANES), F32),
            pltpu.VMEM((2, blocks * GROUP // 2, LANES), F32),
            pltpu.VMEM((2, zh_n, plane * GROUP // 2, LANES), BF16),
            pltpu.VMEM((2, zh_n, plane * GROUP // 2, LANES), BF16),
            pltpu.VMEM((x_n, y_n, share, LANES), BF16),
            pltpu.VMEM((x_n, zl_n * x_share, LANES), BF16),
            pltpu.VMEM((zl_n, width, channels), BF16),
            pltpu.VMEM((zl_n, y_n, x_n, width, x_share), BF16),
            pltpu.VMEM((x_n, outputs, LANES), F32),
            pltpu.VMEM((x_n, outputs, LANES), F32),
            pltpu.VMEM((x_n - 1, outputs, LANES), BF16),
            pltpu.VMEM((x_n - 1, outputs, LANES), BF16),
            dma((11,)),
            dma((plane, 2)),
            dma((plane, 2)),
            dma((plane,)),
            dma((plane,)),
            dma((zh_n, 2)),
            dma((zh_n, 2)),
            dma((3,)),
            dma((zl_n, 2)),
            dma((zl_n,)),
            dma((zl_n, plane)),
            dma((zl_n, plane)),
            dma((zh_n, 2)),
            dma((zh_n, 2)),
            dma((x_n, zl_n, y_n)),
            dma((x_n, zl_n, y_n)),
            dma((x_n,)),
            dma((x_n,)),
            dma((x_n - 1,)),
            dma((x_n - 1,)),
        ],
        compiler_params=pltpu.CompilerParams(
            collective_id=0, has_side_effects=True, vmem_limit_bytes=60 * 1024 * 1024
        ),
        name="hyena_mixer",
    )(
        query_gate,
        key_gate,
        value_input,
        long_filter,
        skip_gain.reshape(1, channels),
        out_weight.T,
        out_bias.reshape(1, -1),
        *tables,
    )


def solution(mesh, dims=(4, 4, 4, 4)):
    placed = (
        P("tp", "ctx"),
        P("tp", "ctx"),
        P("tp", "ctx"),
        P("tp", "ctx"),
        P("tp"),
        P("tp", "ctx"),
        P("tp"),
    )
    return jax.shard_map(
        functools.partial(on_device, dims),
        mesh=mesh,
        in_specs=placed,
        out_specs=P("tp", "ctx"),
        check_vma=False,
    )
```

```python
import functools

import jax
import jax.numpy as jnp
import numpy as np
from jax import lax
from jax.experimental import pallas as pl
from jax.experimental.pallas import tpu as pltpu
from jax.sharding import PartitionSpec as P

F32 = jnp.float32
BF16 = jnp.bfloat16
MESH = pl.DeviceIdType.MESH
LANES = 128
GROUP = 8


def split_bf16(array):
    high = array.astype(BF16)
    low = (array - np.asarray(high, np.float64)).astype(BF16)
    return np.asarray(high), np.asarray(low)


def transform_tables(blocks):
    n1 = np.arange(blocks)[:, None]
    k1 = np.arange(blocks)[None, :] + 0.5
    outer = 2.0 * np.pi * n1 * k1 / (2 * blocks)
    first = np.concatenate([np.cos(outer).T, -np.sin(outer).T], 0)
    first_hi, first_lo = split_bf16(first)
    scale = 2.0 / (2 * blocks * LANES)
    last = np.concatenate([np.cos(outer), -np.sin(outer)], 1) * scale
    last_hi, last_lo = split_bf16(last)
    lane = np.arange(LANES)
    inner = 2.0 * np.pi * (lane[:, None] * lane[None, :] % LANES) / LANES
    cos_part, sin_part = np.cos(inner), -np.sin(inner)
    forward = np.block([[cos_part, sin_part], [-sin_part, cos_part]])
    backward = np.block([[cos_part, -sin_part], [sin_part, cos_part]])
    turn = 2.0 * np.pi * k1.T * lane[None, :] / (2 * blocks * LANES)
    return (
        np.concatenate([first_hi, first_lo], 1),
        np.stack(split_bf16(forward)),
        np.stack(split_bf16(backward)),
        np.concatenate([last_hi, last_lo, last_hi], 1),
        np.stack([np.cos(turn), -np.sin(turn)]).astype(np.float32),
    )


def dot(left, right):
    return jnp.dot(left, right, preferred_element_type=F32)


def halves(value):
    high = value.astype(BF16)
    return high, (value - high.astype(F32)).astype(BF16)


def dot_split(value, table_ref):
    high, low = halves(value)
    return dot(high, table_ref[0]) + dot(low, table_ref[0]) + dot(high, table_ref[1])


def low_high(low, high, swap_low, swap_high):
    row = lax.broadcasted_iota(jnp.int32, low.shape, low.ndim - 2)
    low = pltpu.roll(low, GROUP // 2, low.ndim - 2) if swap_low else low
    high = pltpu.roll(high, GROUP // 2, high.ndim - 2) if swap_high else high
    return jnp.where(row < GROUP // 2, low, high)


def column(row, targets):
    lanes = lax.broadcasted_iota(jnp.int32, (targets.shape[0], row.shape[1]), 1)
    return jnp.sum(jnp.where(lanes == targets, row, 0.0), axis=1, keepdims=True)


def kernel(
    dims,
    q_hbm,
    k_hbm,
    v_hbm,
    h_hbm,
    skip_hbm,
    w_hbm,
    bias_hbm,
    first_hbm,
    fwd_hbm,
    bwd_hbm,
    last_hbm,
    turn_hbm,
    out_ref,
    k_ref,
    v_ref,
    h_ref,
    skip_ref,
    bias_ref,
    first_ref,
    fwd_ref,
    bwd_ref,
    last_ref,
    turn_ref,
    cut,
    rows_in,
    query_in,
    line_cut,
    seq_in,
    direct,
    long_conv,
    wide,
    conv_wide,
    conv_out,
    conv_in,
    gated_out,
    gated,
    w_line,
    weights,
    pair_out,
    pair_in,
    sum_out,
    sum_in,
    load_sem,
    s_send,
    s_recv,
    q_send,
    q_recv,
    z_send,
    z_recv,
    wz_send,
    wf_send,
    w_recv,
    wp_send,
    wp_recv,
    r_send,
    r_recv,
    g_send,
    g_recv,
    c_send,
    c_recv,
    e_send,
    e_recv,
):
    zh_n, y_n, x_n, zl_n = dims
    plane = y_n * x_n
    blocks = zh_n * plane
    me = lax.axis_index("ctx")
    tp = lax.axis_index("tp")
    place = me % plane
    x = me % x_n
    y = place // x_n
    zh = me // plane
    core = tp % 2
    zl = tp // 2
    channels = k_hbm.shape[0]
    x_share = channels // x_n
    share = channels // plane
    width = w_hbm.shape[0]

    def device(zh_at, y_at, x_at, zl_at, core_at=None):
        core_at = core if core_at is None else core_at
        return {"ctx": (zh_at * y_n + y_at) * x_n + x_at, "tp": zl_at * 2 + core_at}

    def in_plane(step):
        return {"ctx": zh * plane + (place + step) % plane, "tp": tp}

    def at_zh(step):
        return device((zh + step) % zh_n, y, x, zl)

    def at_x(step):
        return device(zh, y, (x + step) % x_n, zl)

    def at_y(step):
        return device(zh, (y + step) % y_n, x, zl)

    def at_row(y_step, z_step):
        return device(zh, (y + y_step) % y_n, x, (zl + z_step) % zl_n)

    other_core = {"ctx": me, "tp": zl * 2 + 1 - core}

    def remote(src, dst, send, recv, target):
        return pltpu.make_async_remote_copy(
            src_ref=src, dst_ref=dst, send_sem=send, recv_sem=recv, device_id=target, device_id_type=MESH
        )

    own_rows = pl.ds(pl.multiple_of(x * x_share + y * share, share), share)
    pairs = (
        (k_hbm, k_ref),
        (v_hbm, v_ref),
        (h_hbm, h_ref),
        (first_hbm, first_ref),
        (turn_hbm, turn_ref),
        (fwd_hbm, fwd_ref),
        (bwd_hbm, bwd_ref),
        (last_hbm, last_ref),
        (q_hbm.at[own_rows], query_in.at[place]),
        (skip_hbm, skip_ref),
        (bias_hbm, bias_ref),
    )
    loads = [pltpu.make_async_copy(src, dst, load_sem.at[n]) for n, (src, dst) in enumerate(pairs)]

    barrier = pltpu.get_barrier_semaphore()

    def greet(target):
        pl.semaphore_signal(barrier, inc=1, device_id=target, device_id_type=MESH)

    diagonal = zl == zh
    apart = (zh - zl + zh_n) % zh_n
    last = zh_n - 1
    far_first = sorted(range(1, zh_n), key=lambda step: -min(step, zh_n - step))

    def direct_piece(part):
        above = jnp.logical_and(apart == 1, zl <= part)
        below = jnp.logical_and(apart == last, zl >= part)
        return jnp.logical_or(apart == 0, jnp.logical_or(above, below))

    for step in far_first:
        greet(at_zh(step))
    for part in range(zl_n):

        @pl.when(jnp.logical_and(zl != part, direct_piece(part)))
        def _():
            greet(device(zl, y, x, part))

    for step in range(1, plane):
        greet(in_plane(step))
    for z_step in range(1, zl_n):
        for y_step in range(y_n):
            greet(at_row(y_step, z_step))
    greet(other_core)
    greeted = (zh_n - 1) + (plane - 1) + (zl_n - 1) * y_n + 1

    for load in loads:
        load.start()
    for load in loads[:3]:
        load.wait()
    products = (k_ref[...].astype(F32) * v_ref[...].astype(F32)).reshape(blocks, GROUP, LANES)
    taps = h_ref[...].reshape(blocks, GROUP, LANES)
    pieces = (low_high(products, taps, False, True), low_high(products, taps, True, False))
    for part in range(2):
        packed = pieces[part].reshape(blocks // 2, 2 * GROUP, LANES).astype(BF16)
        for x_at in range(x_n):
            for y_at in range(y_n):
                start = (x_at * y_n + y_at) * zh_n // 2
                cut[part, y_at * x_n + x_at] = packed[start : start + zh_n // 2]
    pl.semaphore_wait(barrier, greeted + jnp.where(diagonal, 0, 2))

    def own_piece(slot, step):
        return remote(
            w_hbm, w_line.at[zl], wz_send.at[slot], w_recv.at[zl], device((zh + step) % zh_n, y, x, zh)
        )

    source_copies = (
        (zl >= zh, own_piece(0, 1)),
        (zl <= zh, own_piece(1, last)),
        (jnp.logical_not(diagonal), own_piece(2, 0)),
    )
    stay = pltpu.make_async_copy(w_hbm, w_line.at[zl], w_recv.at[zl])
    for when, copy in source_copies:

        @pl.when(when)
        def _():
            copy.start()

    @pl.when(diagonal)
    def _():
        stay.start()

    s_copies = []
    for part in range(2):
        sent = []
        for step in range(1, plane):
            copy = remote(
                cut.at[part, (place + step) % plane],
                rows_in.at[part, :, place],
                s_send.at[step, part],
                s_recv.at[step, part],
                in_plane(step),
            )
            copy.start()
            sent.append(copy)
        s_copies.append(sent)

    def relay(part, step, slot, rows=slice(None)):
        piece = w_line.at[part, rows]
        return remote(piece, piece, wf_send.at[slot[0], slot[1]], w_recv.at[part], at_zh(step))

    relay_copies = []
    inner_copies = []
    for part in range(zl_n):
        inner = jnp.logical_and(apart == 0, zl != part)
        for up in range(2):
            step = 1 if up else last
            side = (zl > part) if up else (zl < part)
            inner_copies.append((jnp.logical_and(inner, side), relay(part, step, (part, up))))
        for up in range(2):
            step = 1 if up else last
            outer = apart == (1 if up else last)
            side = (zl < part) if up else (zl > part)
            rows = pl.ds(0, width // 2) if up else pl.ds(width // 2, width // 2)
            relay_copies.append((jnp.logical_and(outer, side), relay(part, step, (part, up))))
            relay_copies.append(
                (jnp.logical_and(outer, zl == part), relay(part, step, (part, up), rows))
            )

    relay_copies += inner_copies
    wp_copies = []
    for part in range(zl_n):
        sent = []
        for step in range(1, plane):
            columns = pl.ds(pl.multiple_of((place + step) % plane % x_n * x_share, x_share), x_share)
            sent.append(
                remote(
                    w_line.at[part, :, columns],
                    weights.at[part, y, x],
                    wp_send.at[part, step],
                    wp_recv.at[part, step],
                    in_plane(step),
                )
            )
        wp_copies.append(sent)

    def piece_in(part):
        pltpu.make_async_copy(w_line.at[part], w_line.at[part], w_recv.at[part]).wait()

    def hand_on(part):
        for copy in wp_copies[part]:
            copy.start()
        columns = pl.ds(pl.multiple_of(x * x_share, x_share), x_share)
        weights[part, y, x] = w_line[part, :, columns]

    for part in range(2):
        rows_in[part, :, pl.ds(place, 1)] = cut[part, pl.ds(place, 1)].reshape(
            zh_n // 2, 1, 2 * GROUP, LANES
        )
    for load in loads[3:]:
        load.wait()

    q_copies = []
    for step in range(1, plane):
        target = (place + step) % plane
        rows = pl.ds(
            pl.multiple_of(target % x_n * x_share + target // x_n * share, share), share
        )
        copy = remote(
            q_hbm.at[rows], query_in.at[place], q_send.at[step], q_recv.at[step], in_plane(step)
        )
        copy.start()
        q_copies.append(copy)

    index = lax.broadcasted_iota(jnp.int32, (share, 1), 0)
    skip = column(skip_ref[...], x * x_share + y * share + index).reshape(zh_n, 1, GROUP, 1)
    z_copies = []
    arrived = []
    for part in range(2):
        for copy in s_copies[part]:
            copy.wait_recv()
        value = rows_in[part].astype(F32).reshape(zh_n // 2, plane, 2, GROUP, LANES)
        arrived.append(value)
        for zh_at in range(zh_n):
            line_cut[part, zh_at] = (
                value[zh_at // 2, :, zh_at % 2].reshape(plane // 2, 2 * GROUP, LANES).astype(BF16)
            )
        sent = []
        for step in far_first:
            copy = remote(
                line_cut.at[part, (zh + step) % zh_n],
                seq_in.at[part, zh],
                z_send.at[step, part],
                z_recv.at[step, part],
                at_zh(step),
            )
            copy.start()
            sent.append(copy)
        seq_in[part, pl.ds(zh, 1)] = line_cut[part, pl.ds(zh, 1)]
        z_copies.append(sent)
    for zh_at in range(zh_n):
        first, second = (value[zh_at // 2, :, zh_at % 2] for value in arrived)
        direct[:, zh_at] = skip[zh_at] * low_high(first, second, False, True)
    for part in range(zl_n):

        @pl.when(direct_piece(part))
        def _():
            piece_in(part)

    for when, copy in relay_copies:

        @pl.when(when)
        def _():
            copy.start()

    for part in range(zl_n):

        @pl.when(direct_piece(part))
        def _():
            hand_on(part)

    turn_re = turn_ref[0]
    turn_im = turn_ref[1]
    turn_re2 = jnp.concatenate([turn_re, turn_re], 1)
    turn_im2 = jnp.concatenate([turn_im, turn_im], 1)
    r_copies = []
    for part in range(2):
        for copy in z_copies[part]:
            copy.wait_recv()
        wide[part] = seq_in[part].astype(F32).reshape(blocks * GROUP, LANES)
        group = range(GROUP // 2)
        spread = []
        for channel in group:
            signal = wide[part, pl.ds(channel, blocks, stride=GROUP), :].astype(BF16)
            taps = wide[part, pl.ds(GROUP // 2 + channel, blocks, stride=GROUP), :].astype(BF16)
            both = jnp.concatenate([signal, taps], 1)
            spread.append(dot(first_ref[...], jnp.concatenate([both, both], 0)))
        stacked = []
        for value in spread:
            re, im = value[:blocks], value[blocks:]
            turned_re = re * turn_re2 - im * turn_im2
            turned_im = re * turn_im2 + im * turn_re2
            stacked.append(jnp.concatenate([turned_re[:, :LANES], turned_im[:, :LANES]], 1))
            stacked.append(jnp.concatenate([turned_re[:, LANES:], turned_im[:, LANES:]], 1))
        spectra = dot_split(jnp.concatenate(stacked, 0), fwd_ref)
        mixed = []
        for channel in group:
            one = spectra[2 * channel * blocks : (2 * channel + 1) * blocks]
            two = spectra[(2 * channel + 1) * blocks : (2 * channel + 2) * blocks]
            s_re, s_im, t_re, t_im = one[:, :LANES], one[:, LANES:], two[:, :LANES], two[:, LANES:]
            mixed.append(jnp.concatenate([s_re * t_re - s_im * t_im, s_re * t_im + s_im * t_re], 1))
        back = dot_split(jnp.concatenate(mixed, 0), bwd_ref)
        unturned = []
        for channel in group:
            one = back[channel * blocks : (channel + 1) * blocks]
            b_re, b_im = one[:, :LANES], one[:, LANES:]
            unturned.append(
                jnp.concatenate([b_re * turn_re + b_im * turn_im, b_im * turn_re - b_re * turn_im], 0)
            )
        for channel in range(0, GROUP // 2, 2):
            high, low = halves(jnp.concatenate(unturned[channel : channel + 2], 1))
            result = dot(last_ref[...], jnp.concatenate([high, high, low], 0))
            conv_wide[part, pl.ds(channel, blocks, stride=GROUP // 2), :] = result[:, :LANES]
            conv_wide[part, pl.ds(channel + 1, blocks, stride=GROUP // 2), :] = result[:, LANES:]
        conv_out[part] = conv_wide[part].reshape(zh_n, plane * GROUP // 2, LANES).astype(BF16)
        for step in far_first:
            copy = remote(
                conv_out.at[part, (zh + step) % zh_n],
                conv_in.at[part, zh],
                r_send.at[step, part],
                r_recv.at[step, part],
                at_zh(step),
            )
            copy.start()
            r_copies.append(copy)
        conv_in[part, pl.ds(zh, 1)] = conv_out[part, pl.ds(zh, 1)]

    for part in range(zl_n):

        @pl.when(jnp.logical_not(direct_piece(part)))
        def _():
            piece_in(part)
            hand_on(part)

    for copy in q_copies:
        copy.wait_recv()
    for copy in r_copies:
        copy.wait_recv()
    first, second = (
        conv_in[part].astype(F32).reshape(zh_n, plane // 2, GROUP, LANES) for part in range(2)
    )
    for spot in range(plane):
        odd = spot % 2 == 1
        long_conv[spot] = direct[spot] + low_high(first[:, spot // 2], second[:, spot // 2], odd, not odd)

    line_rows = pl.ds(pl.multiple_of(zl * x_share + y * share, share), share)
    offsets = sorted(range(1, x_n), key=lambda step: -min(step, x_n - step)) + [0]
    g_copies = []
    for turn, offset in enumerate(offsets):
        at = (x + offset) % x_n
        for y_at in range(y_n):
            spot = y_at * x_n + at
            query = query_in[spot].astype(F32)
            gated_out[turn, y_at] = (query * long_conv[spot].reshape(share, LANES)).astype(BF16)
        sent = []
        for z_step in range(zl_n):
            for y_step in range(y_n):
                if z_step == 0 and y_step == 0:
                    continue
                copy = remote(
                    gated_out.at[turn, (y + y_step) % y_n],
                    gated.at[turn, line_rows],
                    g_send.at[turn, z_step, y_step],
                    g_recv.at[turn, z_step, y_step],
                    at_row(y_step, z_step),
                )
                copy.start()
                sent.append(copy)
        gated[turn, line_rows] = gated_out[turn, y]
        g_copies.append(sent)
    index = lax.broadcasted_iota(jnp.int32, (bias_ref.shape[1], 1), 0)
    bias = column(bias_ref[...], index)
    for sent in wp_copies:
        for copy in sent:
            copy.wait_recv()

    half = y_n // 2

    def project(target, turn):
        blocks_at = pl.ds(target * half, half)
        block = jnp.concatenate(
            [weights[part, blocks_at].reshape(half * x_n * width, x_share) for part in range(zl_n)], 1
        )
        return dot(block, gated[turn])

    c_copies = []
    e_copies = []
    for turn in range(x_n):
        for copy in g_copies[turn]:
            copy.wait_recv()
        pair_out[turn] = project(1 - core, turn)
        pair_copy = remote(
            pair_out.at[turn], pair_in.at[turn], c_send.at[turn], c_recv.at[turn], other_core
        )
        pair_copy.start()
        c_copies.append(pair_copy)
        total = project(core, turn)
        pair_copy.wait_recv()
        total = total + pair_in[turn]
        if turn < x_n - 1:
            sum_out[turn] = total.astype(BF16)
            copy = remote(
                sum_out.at[turn], sum_in.at[turn], e_send.at[turn], e_recv.at[turn], at_x(offsets[turn])
            )
            copy.start()
            e_copies.append(copy)
    total = total + bias
    for turn in range(x_n - 1):
        e_copies[turn].wait_recv()
        total = total + sum_in[turn].astype(F32)
    out_ref[...] = total.astype(BF16)
    for copies in (*s_copies, *z_copies, q_copies, r_copies, *wp_copies, c_copies, e_copies):
        for copy in copies:
            copy.wait_send()

    for when, copy in source_copies + tuple(relay_copies):

        @pl.when(when)
        def _():
            copy.wait_send()

    for sent in g_copies:
        for copy in sent:
            copy.wait_send()


def on_device(dims, query_gate, key_gate, value_input, long_filter, skip_gain, out_weight, out_bias):
    zh_n, y_n, x_n, zl_n = dims
    plane = y_n * x_n
    blocks = zh_n * plane
    channels = key_gate.shape[0]
    width = out_weight.shape[1]
    x_share = channels // x_n
    share = channels // plane
    outputs = out_bias.shape[0]
    tables = [jnp.asarray(table) for table in transform_tables(blocks)]
    dma = pltpu.SemaphoreType.DMA
    return pl.pallas_call(
        functools.partial(kernel, dims),
        out_shape=jax.ShapeDtypeStruct((outputs, LANES), BF16),
        in_specs=[pl.BlockSpec(memory_space=pltpu.HBM)] * 12,
        out_specs=pl.BlockSpec(memory_space=pltpu.VMEM),
        scratch_shapes=[
            pltpu.VMEM((channels, LANES), BF16),
            pltpu.VMEM((channels, LANES), BF16),
            pltpu.VMEM((channels, LANES), F32),
            pltpu.VMEM((1, channels), F32),
            pltpu.VMEM((1, outputs), F32),
            *[pltpu.VMEM(table.shape, table.dtype) for table in tables],
            pltpu.VMEM((2, plane, zh_n // 2, 2 * GROUP, LANES), BF16),
            pltpu.VMEM((2, zh_n // 2, plane, 2 * GROUP, LANES), BF16),
            pltpu.VMEM((plane, share, LANES), BF16),
            pltpu.VMEM((2, zh_n, plane // 2, 2 * GROUP, LANES), BF16),
            pltpu.VMEM((2, zh_n, plane // 2, 2 * GROUP, LANES), BF16),
            pltpu.VMEM((plane, zh_n, GROUP, LANES), F32),
            pltpu.VMEM((plane, zh_n, GROUP, LANES), F32),
            pltpu.VMEM((2, blocks * GROUP, LANES), F32),
            pltpu.VMEM((2, blocks * GROUP // 2, LANES), F32),
            pltpu.VMEM((2, zh_n, plane * GROUP // 2, LANES), BF16),
            pltpu.VMEM((2, zh_n, plane * GROUP // 2, LANES), BF16),
            pltpu.VMEM((x_n, y_n, share, LANES), BF16),
            pltpu.VMEM((x_n, zl_n * x_share, LANES), BF16),
            pltpu.VMEM((zl_n, width, channels), BF16),
            pltpu.VMEM((zl_n, y_n, x_n, width, x_share), BF16),
            pltpu.VMEM((x_n, outputs, LANES), F32),
            pltpu.VMEM((x_n, outputs, LANES), F32),
            pltpu.VMEM((x_n - 1, outputs, LANES), BF16),
            pltpu.VMEM((x_n - 1, outputs, LANES), BF16),
            dma((11,)),
            dma((plane, 2)),
            dma((plane, 2)),
            dma((plane,)),
            dma((plane,)),
            dma((zh_n, 2)),
            dma((zh_n, 2)),
            dma((3,)),
            dma((zl_n, 2)),
            dma((zl_n,)),
            dma((zl_n, plane)),
            dma((zl_n, plane)),
            dma((zh_n, 2)),
            dma((zh_n, 2)),
            dma((x_n, zl_n, y_n)),
            dma((x_n, zl_n, y_n)),
            dma((x_n,)),
            dma((x_n,)),
            dma((x_n - 1,)),
            dma((x_n - 1,)),
        ],
        compiler_params=pltpu.CompilerParams(
            collective_id=0, has_side_effects=True, vmem_limit_bytes=60 * 1024 * 1024
        ),
        name="hyena_mixer",
    )(
        query_gate,
        key_gate,
        value_input,
        long_filter,
        skip_gain.reshape(1, channels),
        out_weight.T,
        out_bias.reshape(1, -1),
        *tables,
    )


def solution(mesh, dims=(4, 4, 4, 4)):
    placed = (
        P("tp", "ctx"),
        P("tp", "ctx"),
        P("tp", "ctx"),
        P("tp", "ctx"),
        P("tp"),
        P("tp", "ctx"),
        P("tp"),
    )
    return jax.shard_map(
        functools.partial(on_device, dims),
        mesh=mesh,
        in_specs=placed,
        out_specs=P("tp", "ctx"),
        check_vma=False,
    )
```
